512 devices in a mesh: section: 16 (over y, z_lo), tile: 32 (over x, z_hi, core).
Axes of the slice: x: 4, y: 8, z: 8 (z_hi: 4, z_lo: 2; z = z_hi * 2 + z_lo), core: 2. Of those that a mesh axis runs over, the one named last changes fastest.
Arguments:
- acts: float32 [16, 1, 256, 16, 256], P('section', None, 'tile')
- kernels: float32 [16, 3, 3, 256, 256], P('section'), may hold values from -0.125 to 0.125
- gammas: float32 [16, 256], P('section'), may hold values from 0.5 to 1.5
- pass_mask: int32 [16, 1, 256, 16, 256], P('section', None, 'tile'), may hold values 0 or 1
- drop_mask: int32 [16, 1, 256, 16], P('section', None, 'tile'), may hold values 0 or 1
- path_mask: int32 [16, 1], P('section'), may hold values from 0 to 1, as said below
- cotangent: float32 [1, 256, 16, 256], P(None, 'tile')
Outputs:
- act_grads: float32 [16, 1, 256, 16, 256], P('section', None, 'tile')
- kernel_grads: float32 [16, 3, 3, 256, 256], P('section', None, None, None, 'tile')
- gain_grads: float32 [16, 2, 256], P('section')
The draws below stay inside these ranges and needn't reach their ends.
Inputs may be any that keep to these rules, and one draw needn't show every extreme that they name: `path_mask`: both values occur among the 16 entries.
All inputs are finite; a program needn't handle non-finite values. No bound on the sum of `pass_mask` or of `drop_mask` on one device may be relied on, other than what follows from the above.
Results may differ from the reference program's by a relative error of at most 0.00014.
Values sent between devices are 32-bit elements; how exact they have to be, the bound alone decides.
No kernel may reach another device: no remote copies, remote signals or barrier semaphores. Data moves between devices by JAX's collectives and lax.ppermute only.
A program may use at most 64 MiB of HBM per device.

```python
import jax
import jax.numpy as jnp
from jax import lax

C = 256
GROUPS = 32
COLS = 16
MICRO = 1
SECTIONS = 16
HEIGHT = 256


def shaped_field(key, shape):
    rising = 1.0 + 2.0 * jnp.arange(HEIGHT, dtype=jnp.float32) / (HEIGHT - 1)
    rising = rising[:, None, None]
    return jax.random.normal(key, shape, jnp.float32) * rising


def draw_acts(key, part):
    key = jax.random.fold_in(key, 11)
    return shaped_field(key, (SECTIONS, MICRO, HEIGHT, COLS, C))


def draw_cotangent(key, part):
    key = jax.random.fold_in(key, 12)
    return shaped_field(key, (MICRO, HEIGHT, COLS, C))


def draw_path_mask(key, part):
    key = jax.random.fold_in(key, 13)
    total = SECTIONS * MICRO
    dropped = max(1, total // 4)
    order = jax.random.permutation(key, total)
    kept = (order < total - dropped).astype(jnp.int32)
    return kept.reshape((SECTIONS, MICRO))


def with_ends(entries, stream_key, least, largest):
    longest = entries.shape.index(max(entries.shape))
    spots = []
    for shift in (0, 1):
        where = [jax.random.randint(jax.random.fold_in(stream_key, axis), (), 0, length) for axis, length in enumerate(entries.shape)]
        where[longest] = (where[longest] + shift) % entries.shape[longest]
        spots.append(tuple(where))
    return entries.at[spots[0]].set(least).at[spots[1]].set(largest)


def level_of(key, shape, cuts, low, high):
    def one(position, shards_of):
        heights = jax.random.uniform(jax.random.fold_in(jax.random.fold_in(key, 6), position), (shards_of,), jnp.float32, low / len(cuts), high / len(cuts))
        return jnp.repeat(jnp.exp(heights), shape[position] // shards_of).reshape((-1,) + (1,) * (len(shape) - position - 1))

    gain = one(*cuts[0])
    for cut in cuts[1:]:
        gain = gain * one(*cut)
    return gain


def bell_draw(rng, dims, deviation, limit, cuts=(), kind=jnp.bfloat16):
    result = jax.random.normal(rng, dims, jnp.float32) * deviation
    if len(cuts) > 0:
        result = level_of(rng, dims, cuts, -0.22, 0.18) * result
    return jnp.clip(result, min=-limit, max=limit).astype(kind)


def setup_inputs(seed: int = 0) -> dict:
    splits = jax.random.split(jax.random.key(seed), 8)
    return {
        "acts": draw_acts(jax.random.fold_in(splits[7], 71), 0),
        "kernels": bell_draw(splits[1], (SECTIONS, 3, 3, C, C), (9 * C) ** -0.5, 0.125, ((0, 16),), jnp.float32),
        "gammas": jnp.clip(0.5 + 1.0 * jax.random.uniform(splits[2], (SECTIONS, C), jnp.float32) ** level_of(splits[2], (SECTIONS, C), ((0, 16),), -0.2, 0.2), 0.5, 1.5),
        "pass_mask": with_ends((jax.random.randint(splits[3], (SECTIONS, MICRO, HEIGHT, COLS, C), 0, 2) < 1).astype(jnp.int32), jax.random.fold_in(splits[3], 1), 0, 1),
        "drop_mask": with_ends((jax.random.randint(splits[4], (SECTIONS, MICRO, HEIGHT, COLS), 0, 10) < 9).astype(jnp.int32), jax.random.fold_in(splits[4], 1), 0, 1),
        "path_mask": draw_path_mask(jax.random.fold_in(splits[7], 71), 0),
        "cotangent": draw_cotangent(jax.random.fold_in(splits[7], 71), 0),
    }


keep_drop = 0.9
keep_path = 0.75
eps = 1e-05
highest = lax.Precision.HIGHEST

def conv_apply(padded, kernel, row_count, col_count):
    summed = None
    for row_tap in range(3):
        for col_tap in range(3):
            window = padded[:, row_tap:row_tap + row_count, col_tap:col_tap + col_count]
            product = jnp.einsum('mhwc,cd->mhwd', window, kernel[row_tap, col_tap], precision=highest)
            summed = product if summed is None else summed + product
    return summed

def group_sums(values):
    shaped = values.reshape(values.shape[:3] + (GROUPS, values.shape[3] // GROUPS))
    return lax.optimization_barrier(jnp.sum(shaped, axis=(1, 2, 4)))

def spread_groups(group_values, channels):
    return jnp.repeat(group_values, channels // group_values.shape[1], axis=1)[:, None, None, :]

def reference(acts, kernels, gammas, pass_mask, drop_mask, path_mask, cotangent):
    group_count = HEIGHT * COLS * (C // GROUPS)
    gradient = cotangent
    act_list = []
    kernel_list = []
    gain_list = []
    for layer_index in reversed(range(SECTIONS)):
        inputs = acts[layer_index]
        kernel = kernels[layer_index]
        padded = jnp.pad(inputs, ((0, 0), (1, 1), (1, 1), (0, 0)))
        conv_out = conv_apply(padded, kernel, HEIGHT, COLS)
        group_mean = group_sums(conv_out) / group_count
        square_mean = group_sums(conv_out * conv_out) / group_count
        inverse_std = lax.rsqrt(square_mean - group_mean * group_mean + eps)
        normed = (conv_out - spread_groups(group_mean, C)) * spread_groups(inverse_std, C)
        passing = pass_mask[layer_index].astype(jnp.float32) * (drop_mask[layer_index].astype(jnp.float32)[..., None] / keep_drop) * (path_mask[layer_index].astype(jnp.float32)[:, None, None, None] / keep_path)
        grad_out = gradient * passing
        gain_list.append(jnp.stack([lax.optimization_barrier(jnp.sum(grad_out * normed, axis=(0, 1, 2))), lax.optimization_barrier(jnp.sum(grad_out, axis=(0, 1, 2)))]))
        grad_norm = grad_out * gammas[layer_index]
        first_mean = group_sums(grad_norm) / group_count
        cross_mean = group_sums(grad_norm * normed) / group_count
        grad_conv = spread_groups(inverse_std, C) * (grad_norm - spread_groups(first_mean, C) - normed * spread_groups(cross_mean, C))
        kernel_grad = jnp.stack([jnp.stack([jnp.einsum('mhwc,mhwd->cd', padded[:, row_tap:row_tap + HEIGHT, col_tap:col_tap + COLS], grad_conv, precision=highest) for col_tap in range(3)]) for row_tap in range(3)])
        kernel_list.append(kernel_grad)
        flipped = jnp.transpose(kernel[::-1, ::-1], (0, 1, 3, 2))
        padded_grad = jnp.pad(grad_conv, ((0, 0), (1, 1), (1, 1), (0, 0)))
        gradient = gradient + conv_apply(padded_grad, flipped, HEIGHT, COLS)
        act_list.append(gradient)
    return (jnp.stack(act_list[::-1]), jnp.stack(kernel_list[::-1]), jnp.stack(gain_list[::-1]))
```

```python
import functools

import jax
import jax.numpy as jnp
from jax import lax
from jax.experimental import pallas as pl
from jax.experimental.pallas import tpu as pltpu
from jax.sharding import Mesh
from jax.sharding import PartitionSpec as P

GROUPS = 32
C = 256
COLS = 16
ROWS = 8
OWN = ROWS * COLS

keep_drop = 0.9
keep_path = 0.75
eps = 1e-05
highest = lax.Precision.HIGHEST
f32 = jnp.float32
bf16 = jnp.bfloat16

SECTION = ("pair", "member")
TILE = ("x", "z", "core")
ALL = SECTION + TILE


def split(values):
    high = values.astype(bf16)
    return high, (values - high.astype(f32)).astype(bf16)


def dot(left, right, precision=None):
    return jnp.dot(left, right, preferred_element_type=f32, precision=precision)


def dot3(left, right):
    lh, ll = left
    rh, rl = right
    return dot(lh, rh) + dot(ll, rh) + dot(lh, rl)


def shifted(values, offset):
    if offset == 0:
        return values
    count = values.shape[0]
    column = lax.broadcasted_iota(jnp.int32, values.shape, 0) & (COLS - 1)
    rolled = pltpu.roll(values, (-offset) % count, 0)
    edge = COLS - 1 if offset > 0 else 0
    return jnp.where(column == edge, 0.0, rolled)


def conv_back(field, high_ref, low_ref):
    wide = jnp.concatenate([shifted(field, 1), field, shifted(field, -1)], axis=1)
    high, low = split(wide)
    count = field.shape[0] - 2 * COLS
    total = None
    for tap in range(3):
        start = (2 - tap) * COLS
        part = dot3(
            (high[start : start + count], low[start : start + count]),
            (high_ref[tap], low_ref[tap]),
        )
        total = part if total is None else total + part
    return total


def group_matrix():
    channel = lax.broadcasted_iota(jnp.int32, (C, GROUPS), 0)
    group = lax.broadcasted_iota(jnp.int32, (C, GROUPS), 1)
    return jnp.where((channel >> 3) == group, 1.0, 0.0).astype(f32)


def spread_matrix():
    channel = lax.broadcasted_iota(jnp.int32, (GROUPS, C), 1)
    group = lax.broadcasted_iota(jnp.int32, (GROUPS, C), 0)
    return jnp.where((channel >> 3) == group, 1.0, 0.0).astype(f32)


def column_sum(values):
    return jnp.sum(values, axis=0, keepdims=True)


def forward_kernel(top, main, bottom, kernel, conv_out, sums):
    image = jnp.concatenate([top[...], main[...], bottom[...]], axis=0)
    count = image.shape[0] - 2 * COLS
    total = None
    for col_tap in range(3):
        high, low = split(shifted(image, col_tap - 1))
        for row_tap in range(3):
            start = row_tap * COLS
            part = dot3(
                (high[start : start + count], low[start : start + count]),
                split(kernel[row_tap * 3 + col_tap]),
            )
            total = part if total is None else total + part
    conv_out[...] = total
    own = total[2 * COLS : 2 * COLS + OWN]
    sums[...] = jnp.concatenate([column_sum(own), column_sum(own * own)], axis=0)


def prepare_kernel(
    flags, own, near, far, pass_b, norm_a, norm_b, valid, scale,
    a_high, a_low, b_high, b_low, response, weight_scr, flat_scr, full_scr,
):
    tap = pl.program_id(0)
    core = flags[3]
    member = flags[1]
    near_tap, far_tap = near[0], far[0]
    partner = jnp.concatenate(
        [jnp.where(core == 0, near_tap, far_tap), jnp.where(core == 0, far_tap, near_tap)], axis=0
    )
    kernel_a = jnp.where(member == 1, own[0], partner)
    kernel_b = jnp.where(member == 1, partner, own[0])
    high, low = split(kernel_a.T)
    a_high[0] = high
    a_low[0] = low
    high, low = split(kernel_b.T)
    b_high[0] = high
    b_low[0] = low

    @pl.when(tap == 0)
    def _():
        passing = pass_b[2 * COLS : 2 * COLS + OWN]
        normed = norm_b[2 * COLS : 2 * COLS + OWN]
        weight_scr[...] = jnp.concatenate([passing.T, (passing * normed).T], axis=0)
        flat_scr[...] = jnp.zeros_like(flat_scr)
        full_scr[...] = jnp.zeros_like(full_scr)

    row_tap = tap // 3
    col_tap = tap - row_tap * 3
    begin = pl.multiple_of((3 - row_tap) * COLS, COLS)
    fields = jnp.concatenate(
        [norm_a[pl.ds(begin, OWN), :], valid[pl.ds(begin, OWN), :]], axis=1
    )
    moved = jnp.where(
        col_tap == 1,
        fields,
        jnp.where(col_tap == 0, shifted(fields, 1), shifted(fields, -1)),
    )
    moment = dot3(split(weight_scr[...]), split(moved))
    both = jnp.concatenate([kernel_a, kernel_a], axis=0)
    full_scr[...] += moment[:, :C] * both
    flat_scr[...] += moment[:, C : C + 1] * both

    @pl.when(tap == 8)
    def _():
        groups = group_matrix()
        contract = (((0,), (1,)), ((), ()))
        for index, scratch in enumerate((flat_scr, full_scr)):
            response[GROUPS * index : GROUPS * (index + 1), :] = lax.dot_general(
                groups, scratch[...] * scale[...], contract,
                preferred_element_type=f32, precision=highest,
            )


def first_kernel(top, main, bottom, pass_a, norm_a, pass_b, norm_b, params, a_high, a_low, sums):
    incoming = jnp.concatenate([top[...], main[...], bottom[...]], axis=0)
    grad_out = incoming * pass_a[...]
    own = slice(2 * COLS, 2 * COLS + OWN)
    scaled = grad_out[COLS:-COLS] * (params[0:1, :] * params[1:2, :])
    rest = incoming[own] + conv_back(scaled, a_high, a_low)
    grad_b = rest * pass_b[own, :]
    parts = jnp.concatenate(
        [
            column_sum(grad_out[own]),
            column_sum(grad_out[own] * norm_a[own, :]),
            column_sum(grad_b),
            column_sum(grad_b * norm_b[own, :]),
        ],
        axis=0,
    )
    sums[...] = jnp.broadcast_to(parts[None], sums.shape)


def second_kernel(
    count, flags, received, response, top, main, bottom, pass_a, norm_a, pass_b, norm_b, valid,
    params, a_high, a_low, b_high, b_low, old_act, old_grad, old_gain,
    out, out_head, out_tail, act, grad, gain,
):
    incoming = jnp.concatenate([top[...], main[...], bottom[...]], axis=0)
    gamma_a, inverse_a, gamma_b, inverse_b = (params[i : i + 1, :] for i in range(4))
    totals = jnp.sum(received[...], axis=0)
    groups, spread = group_matrix(), spread_matrix()
    means_a = dot(totals[0:2] * gamma_a, groups, highest) * (1.0 / count)
    shift = dot(means_a[0:1], response[:GROUPS, :], highest) + dot(
        means_a[1:2], response[GROUPS:, :], highest
    )
    totals_b = totals[2:4] - jnp.concatenate([shift[:, :C], shift[:, C:]], axis=0)
    means_b = dot(totals_b * gamma_b, groups, highest) * (1.0 / count)
    wide_a = dot(means_a, spread, highest)
    wide_b = dot(means_b, spread, highest)
    inside = jnp.concatenate([valid[...], valid[...]], axis=1)
    grad_a = inverse_a * (
        incoming * pass_a[...] * gamma_a - inside * wide_a[0:1] - norm_a[...] * wide_a[1:2]
    )
    middle = incoming[COLS:-COLS] + conv_back(grad_a, a_high, a_low)
    grad_b = inverse_b * (
        middle * pass_b[COLS:-COLS, :] * gamma_b
        - inside[COLS:-COLS] * wide_b[0:1]
        - norm_b[COLS:-COLS, :] * wide_b[1:2]
    )
    last = middle[COLS:-COLS] + conv_back(grad_b, b_high, b_low)
    out[...] = last
    out_head[...] = last[: 2 * COLS]
    out_tail[...] = last[-2 * COLS :]
    active = flags[0] == 1
    upper = flags[1] == 1
    act[...] = jnp.where(
        active, jnp.where(upper, middle[COLS:-COLS], last), old_act[...]
    )
    grad[...] = jnp.where(
        active, jnp.where(upper, grad_a[2 * COLS : -2 * COLS], grad_b[COLS:-COLS]), old_grad[...]
    )
    pair_a = jnp.concatenate([totals[1:2], totals[0:1]], axis=0)
    pair_b = jnp.concatenate([totals_b[1:2], totals_b[0:1]], axis=0)
    gain[...] = jnp.where(active, jnp.where(upper, pair_a, pair_b), old_gain[...])


def kernel_grad_kernel(tiles, flags, top, main, bottom, grad, mine, other):
    share = C // tiles
    image = jnp.concatenate([top[...], main[...], bottom[...]], axis=0)
    turned = grad[...].T.reshape(tiles // 2, 2, share, OWN)
    even = turned[:, 0].reshape(C // 2, OWN)
    odd = turned[:, 1].reshape(C // 2, OWN)
    core = flags[3]
    left = split(
        jnp.concatenate(
            [jnp.where(core == 0, even, odd), jnp.where(core == 0, odd, even)], axis=0
        )
    )
    for col_tap in range(3):
        high, low = split(shifted(image, col_tap - 1))
        for row_tap in range(3):
            start = (row_tap + 2) * COLS
            product = dot3(left, (high[start : start + OWN], low[start : start + OWN]))
            where = slice((row_tap * 3 + col_tap) * C, (row_tap * 3 + col_tap + 1) * C)
            mine[:, where] = product[: C // 2]
            other[:, where] = product[C // 2 :]


def call(body, out_shape, operands, flagged, **options):
    spec = pl.BlockSpec(memory_space=pltpu.VMEM)
    in_specs = [spec] * len(operands)
    if flagged:
        in_specs[0] = pl.BlockSpec(memory_space=pltpu.SMEM)
    many = isinstance(out_shape, tuple)
    return pl.pallas_call(
        body,
        out_shape=out_shape,
        in_specs=in_specs,
        out_specs=tuple(spec for _ in out_shape) if many else spec,
        compiler_params=pltpu.CompilerParams(vmem_limit_bytes=40 * 2**20),
        **options,
    )(*operands)


def shape(*dims, dtype=f32):
    return jax.ShapeDtypeStruct(dims, dtype)


def prepare(flags, kernel, near, far, pass_b, norm_a, norm_b, valid, scale):
    tap = lambda rows: pl.BlockSpec((1, rows, C), lambda i: (i, 0, 0))
    whole = lambda a: pl.BlockSpec(a.shape, lambda i: (0,) * a.ndim)
    return pl.pallas_call(
        prepare_kernel,
        grid=(9,),
        out_shape=tuple(shape(9, C, C, dtype=bf16) for _ in range(4))
        + (shape(2 * GROUPS, 2 * C),),
        in_specs=[
            pl.BlockSpec(memory_space=pltpu.SMEM),
            tap(C),
            tap(C // 2),
            tap(C // 2),
            whole(pass_b),
            whole(norm_a),
            whole(norm_b),
            whole(valid),
            whole(scale),
        ],
        out_specs=tuple(tap(C) for _ in range(4))
        + (pl.BlockSpec((2 * GROUPS, 2 * C), lambda i: (0, 0)),),
        scratch_shapes=[
            pltpu.VMEM((2 * C, OWN), f32),
            pltpu.VMEM((2 * C, C), f32),
            pltpu.VMEM((2 * C, C), f32),
        ],
        compiler_params=pltpu.CompilerParams(vmem_limit_bytes=40 * 2**20),
    )(flags, kernel, near, far, pass_b, norm_a, norm_b, valid, scale)


def on_device(acts, kernels, gammas, pass_mask, drop_mask, path_mask, cotangent):
    pairs = lax.axis_size("pair")
    tiles = lax.axis_size(TILE)
    devices = 2 * pairs * tiles
    pair, member, core = (lax.axis_index(a) for a in ("pair", "member", "core"))
    tile = lax.axis_index(TILE)
    count = tiles * OWN * (C // GROUPS)
    swap = [(0, 1), (1, 0)]

    own_kernel = kernels[0].reshape(9, C, C)
    half = lax.dynamic_slice_in_dim(own_kernel, core * (C // 2), C // 2, axis=1)
    near = lax.ppermute(half, "member", swap)
    far = lax.ppermute(near, "core", swap)

    passing = (
        pass_mask[0, 0].astype(f32)
        * (drop_mask[0, 0].astype(f32)[..., None] / keep_drop)
        * (path_mask[0].astype(f32)[:, None, None] / keep_path)
    ).reshape(OWN, C)
    image = acts[0, 0].reshape(OWN, C)
    start = cotangent[0].reshape(OWN, C)

    def neighbours(value, step, jump):
        return lax.ppermute(
            value,
            ALL,
            [
                (i, i - jump * 2 * tiles + step)
                for i in range(jump * 2 * tiles, devices)
                if 0 <= i % tiles + step < tiles
            ],
        )

    from_above = neighbours(
        jnp.concatenate([image[-3 * COLS :], passing[-2 * COLS :], start[-2 * COLS :]]), 1, 0
    )
    from_below = neighbours(
        jnp.concatenate([image[: 3 * COLS], passing[: 2 * COLS], start[: 2 * COLS]]), -1, 0
    )
    cuts = (0, 3 * COLS, 5 * COLS, 7 * COLS)
    above = [from_above[a:b] for a, b in zip(cuts, cuts[1:])]
    below = [from_below[a:b] for a, b in zip(cuts, cuts[1:])]
    image_parts = (above[0], image, below[0])
    passing = jnp.concatenate([above[1], passing, below[1]])
    tall = 12 * COLS
    conv_out, sums = call(
        forward_kernel,
        (shape(tall, C), shape(2, C)),
        image_parts + (own_kernel,),
        False,
    )
    fields = jnp.stack([conv_out, passing])
    partner_fields = lax.ppermute(fields, "member", swap)
    packed = jnp.concatenate([sums, gammas, jnp.zeros((1, C), f32)])
    gathered = lax.all_to_all(
        jnp.broadcast_to(packed, (2 * tiles, 4, C)), ("member",) + TILE, 0, 0
    ).reshape(2, tiles, 4, C)
    totals = jnp.sum(gathered[:, :, :2], axis=1)
    gamma_both = gathered[:, 0, 2]
    group_totals = jnp.sum(totals.reshape(2, 2, GROUPS, C // GROUPS), axis=3) / count
    mean = group_totals[:, 0]
    inverse = lax.rsqrt(group_totals[:, 1] - mean * mean + eps)
    mean = jnp.repeat(mean, C // GROUPS, axis=1)
    inverse = jnp.repeat(inverse, C // GROUPS, axis=1)
    row = jnp.arange(tall, dtype=jnp.int32)[:, None]
    inside = ((tile > 0) | (row >= 2 * COLS)) & ((tile < tiles - 1) | (row < 10 * COLS))
    valid = jnp.broadcast_to(inside.astype(f32), (tall, C // 2))
    inside = inside.astype(f32)

    upper = member == 1
    conv_a = jnp.where(upper, fields[0], partner_fields[0])
    conv_b = jnp.where(upper, partner_fields[0], fields[0])
    pass_a = jnp.where(upper, fields[1], partner_fields[1])
    pass_b = jnp.where(upper, partner_fields[1], fields[1])
    norm_a = (conv_a - mean[1:2]) * inverse[1:2] * inside
    norm_b = (conv_b - mean[0:1]) * inverse[0:1] * inside
    params = jnp.concatenate(
        [gamma_both[1:2], inverse[1:2], gamma_both[0:1], inverse[0:1], jnp.zeros((4, C), f32)]
    )

    flags = jnp.stack([pair * 0, member, tile, core]).astype(jnp.int32)
    a_high, a_low, b_high, b_low, response = prepare(
        flags, own_kernel, near, far, pass_b, norm_a, norm_b, valid, inverse[1:2]
    )
    a_high, a_low, b_high, b_low = (
        w.reshape(3, 3 * C, C) for w in (a_high, a_low, b_high, b_low)
    )
    piece = 2 * GROUPS // tiles
    response = jnp.sum(
        lax.all_to_all(response.reshape(tiles, piece, 2 * C), TILE, 0, 0), axis=0
    )
    response_share = jnp.broadcast_to(
        response.reshape(1, 2 * piece, C), (tiles, 2 * piece, C)
    )

    top, main, bottom = above[2], start, below[2]
    act = jnp.zeros((OWN, C), f32)
    grad = jnp.zeros((OWN, C), f32)
    gain = jnp.zeros((2, C), f32)
    response = None
    for step in range(pairs):
        rows = (top, main, bottom)
        masks = (pass_a, norm_a, pass_b, norm_b)
        sums = call(
            first_kernel,
            shape(tiles, 4, C),
            rows + masks + (params, a_high, a_low),
            False,
        )
        if step == 0:
            exchanged = lax.all_to_all(
                jnp.concatenate([sums, response_share], axis=1), TILE, 0, 0
            )
            received = exchanged[:, :4]
            response = exchanged[:, 4:].reshape(2 * GROUPS, 2 * C)
        else:
            received = lax.all_to_all(sums, TILE, 0, 0)
        here = jnp.stack([(pair == pairs - 1 - step).astype(jnp.int32), member, tile, core])
        main, head, tail, act, grad, gain = call(
            functools.partial(second_kernel, count),
            (
                shape(OWN, C),
                shape(2 * COLS, C),
                shape(2 * COLS, C),
                shape(OWN, C),
                shape(OWN, C),
                shape(2, C),
            ),
            (here, received, response)
            + rows
            + masks
            + (valid, params, a_high, a_low, b_high, b_low, act, grad, gain),
            True,
        )
        if step < pairs - 1:
            main, top, bottom = (
                neighbours(main, 0, 1),
                neighbours(tail, 1, 1),
                neighbours(head, -1, 1),
            )

    mine, other = call(
        functools.partial(kernel_grad_kernel, tiles),
        (shape(C // 2, 9 * C), shape(C // 2, 9 * C)),
        (flags,) + image_parts + (grad,),
        True,
    )
    share = C // tiles
    mine = mine + lax.ppermute(other, "core", swap)
    for axis in ("x", "z"):
        parts = lax.axis_size(axis)
        mine = jnp.sum(
            lax.all_to_all(mine.reshape(parts, mine.shape[0] // parts, 9 * C), axis, 0, 0), axis=0
        )
    kernel_share = jnp.transpose(mine.reshape(share, 3, 3, C), (1, 2, 3, 0))
    return (
        act.reshape(1, 1, ROWS, COLS, C),
        kernel_share[None],
        gain[None],
    )


def solution(mesh):
    sections, tiles = mesh.shape["section"], mesh.shape["tile"]
    across = 4 if tiles == 32 else 1
    finer = Mesh(
        mesh.devices.reshape(sections // 2, 2, tiles // (2 * across), across, 2), ALL
    )
    return jax.shard_map(
        on_device,
        mesh=finer,
        in_specs=(
            P(SECTION, None, TILE, None, None),
            P(SECTION, None, None, None, None),
            P(SECTION, None),
            P(SECTION, None, TILE, None, None),
            P(SECTION, None, TILE, None),
            P(SECTION, None),
            P(None, TILE, None, None),
        ),
        out_specs=(
            P(SECTION, None, TILE, None, None),
            P(SECTION, None, None, None, TILE),
            P(SECTION, None, None),
        ),
        check_vma=False,
    )
```

```python
import functools

import jax
import jax.numpy as jnp
from jax import lax
from jax.experimental import pallas as pl
from jax.experimental.pallas import tpu as pltpu
from jax.sharding import Mesh
from jax.sharding import PartitionSpec as P

GROUPS = 32
C = 256
COLS = 16
ROWS = 8
OWN = ROWS * COLS

keep_drop = 0.9
keep_path = 0.75
eps = 1e-05
highest = lax.Precision.HIGHEST
f32 = jnp.float32
bf16 = jnp.bfloat16

SECTION = ("pair", "member")
TILE = ("x", "z", "core")
ALL = SECTION + TILE


def split(values):
    high = values.astype(bf16)
    return high, (values - high.astype(f32)).astype(bf16)


def dot(left, right, precision=None):
    return jnp.dot(left, right, preferred_element_type=f32, precision=precision)


def dot3(left, right):
    lh, ll = left
    rh, rl = right
    return dot(lh, rh) + dot(ll, rh) + dot(lh, rl)


def shifted(values, offset):
    if offset == 0:
        return values
    count = values.shape[0]
    column = lax.broadcasted_iota(jnp.int32, values.shape, 0) & (COLS - 1)
    rolled = pltpu.roll(values, (-offset) % count, 0)
    edge = COLS - 1 if offset > 0 else 0
    return jnp.where(column == edge, 0.0, rolled)


def conv_back(field, high_ref, low_ref):
    wide = jnp.concatenate([shifted(field, 1), field, shifted(field, -1)], axis=1)
    high, low = split(wide)
    count = field.shape[0] - 2 * COLS
    total = None
    for tap in range(3):
        start = (2 - tap) * COLS
        part = dot3(
            (high[start : start + count], low[start : start + count]),
            (high_ref[tap], low_ref[tap]),
        )
        total = part if total is None else total + part
    return total


def group_matrix():
    channel = lax.broadcasted_iota(jnp.int32, (C, GROUPS), 0)
    group = lax.broadcasted_iota(jnp.int32, (C, GROUPS), 1)
    return jnp.where((channel >> 3) == group, 1.0, 0.0).astype(f32)


def spread_matrix():
    channel = lax.broadcasted_iota(jnp.int32, (GROUPS, C), 1)
    group = lax.broadcasted_iota(jnp.int32, (GROUPS, C), 0)
    return jnp.where((channel >> 3) == group, 1.0, 0.0).astype(f32)


def column_sum(values):
    return jnp.sum(values, axis=0, keepdims=True)


def forward_kernel(top, main, bottom, kernel, gamma, conv_out, sums):
    image = jnp.concatenate([top[...], main[...], bottom[...]], axis=0)
    count = image.shape[0] - 2 * COLS
    total = None
    for col_tap in range(3):
        high, low = split(shifted(image, col_tap - 1))
        for row_tap in range(3):
            start = row_tap * COLS
            part = dot3(
                (high[start : start + count], low[start : start + count]),
                split(kernel[row_tap * 3 + col_tap]),
            )
            total = part if total is None else total + part
    conv_out[...] = total
    own = total[2 * COLS : 2 * COLS + OWN]
    block = jnp.concatenate(
        [column_sum(own), column_sum(own * own), gamma[...], jnp.zeros((1, C), f32)], axis=0
    )
    sums[...] = jnp.broadcast_to(folded(block)[None], sums.shape)


def prepare_kernel(
    tiles, count, flags, own, near, far, gathered, fields, partner_fields,
    a_high, a_low, b_high, b_low, pass_a, norm_a, pass_b, norm_b, params, response,
    high_scr, low_scr, field_scr, flat_scr, full_scr,
):
    tap = pl.program_id(0)
    core = flags[3]
    member = flags[1]

    @pl.when(tap == 0)
    def _():
        stats = gathered[...].reshape(2, tiles, 8, C // 2)
        groups, spread = group_matrix(), spread_matrix()
        inside = inside_rows(flags, tiles)

        def section(which, conv_out, passing, pass_ref, norm_ref, row):
            block = jnp.sum(stats[which], axis=0)
            totals = jnp.concatenate([block[0:2], block[4:6]], axis=1)
            gamma = jnp.concatenate([stats[which, 0, 2:3], stats[which, 0, 6:7]], axis=1)
            grouped = dot(totals, groups, highest) * (1.0 / count)
            mean = grouped[0:1]
            inverse = lax.rsqrt(grouped[1:2] - mean * mean + eps)
            wide = dot(jnp.concatenate([mean, inverse], axis=0), spread, highest)
            mean, inverse = wide[0:1], wide[1:2]
            pass_ref[...] = passing
            norm_ref[...] = (conv_out - mean) * inverse * inside
            params[row : row + 1, :] = gamma
            params[row + 1 : row + 2, :] = inverse

        upper = member == 1
        mine, other = fields[0], partner_fields[0]
        my_pass, other_pass = fields[1], partner_fields[1]
        section(1, jnp.where(upper, mine, other), jnp.where(upper, my_pass, other_pass),
                pass_a, norm_a, 0)
        section(0, jnp.where(upper, other, mine), jnp.where(upper, other_pass, my_pass),
                pass_b, norm_b, 2)
        params[4:8, :] = jnp.zeros((4, C), f32)
        passing = pass_b[2 * COLS : 2 * COLS + OWN]
        normed = norm_b[2 * COLS : 2 * COLS + OWN]
        high, low = split(jnp.concatenate([passing.T, (passing * normed).T], axis=0))
        high_scr[...] = high
        low_scr[...] = low
        both = jnp.concatenate([norm_a[...], inside[:, : C // 2]], axis=1)
        field_scr[0] = shifted(both, 1)
        field_scr[1] = both
        field_scr[2] = shifted(both, -1)
        flat_scr[...] = jnp.zeros_like(flat_scr)
        full_scr[...] = jnp.zeros_like(full_scr)

    near_tap, far_tap = near[0], far[0]
    partner = jnp.concatenate(
        [jnp.where(core == 0, near_tap, far_tap), jnp.where(core == 0, far_tap, near_tap)], axis=0
    )
    kernel_a = jnp.where(member == 1, own[0], partner)
    kernel_b = jnp.where(member == 1, partner, own[0])
    high, low = split(kernel_a.T)
    a_high[0] = high
    a_low[0] = low
    high, low = split(kernel_b.T)
    b_high[0] = high
    b_low[0] = low

    row_tap = tap // 3
    col_tap = tap - row_tap * 3
    begin = pl.multiple_of((3 - row_tap) * COLS, COLS)
    moved = split(field_scr[col_tap, pl.ds(begin, OWN), :])
    moment = dot3((high_scr[...], low_scr[...]), moved)
    full_scr[:C, :] += moment[:C, :C] * kernel_a
    full_scr[C:, :] += moment[C:, :C] * kernel_a
    flat_scr[:C, :] += moment[:C, C : C + 1] * kernel_a
    flat_scr[C:, :] += moment[C:, C : C + 1] * kernel_a

    @pl.when(tap == 8)
    def _():
        groups = group_matrix()
        contract = (((0,), (1,)), ((), ()))
        for index, scratch in enumerate((flat_scr, full_scr)):
            part = lax.dot_general(
                groups, scratch[...] * params[1:2, :], contract,
                preferred_element_type=f32, precision=highest,
            )
            for chunk in range(4):
                response[:, index * 4 + chunk, :] = part[:, chunk * 128 : (chunk + 1) * 128]


def inside_rows(flags, tiles):
    row = lax.broadcasted_iota(jnp.int32, (12 * COLS, C), 0)
    first = jnp.where(flags[2] == 0, 2 * COLS, 0)
    last = jnp.where(flags[2] == tiles - 1, 10 * COLS, 12 * COLS)
    return jnp.where((row >= first) & (row < last), 1.0, 0.0).astype(f32)


def folded(values):
    return jnp.concatenate([values[:, : C // 2], values[:, C // 2 :]], axis=0)


def first_sums(main, pass_a, norm_a, pass_b, norm_b, params, a_high, a_low):
    own = slice(2 * COLS, 2 * COLS + OWN)
    incoming = main[...]
    grad_out = incoming * pass_a[own, :]
    blank = jnp.zeros((2 * COLS, C), f32)
    scaled = jnp.concatenate([blank, grad_out * (params[0:1, :] * params[1:2, :]), blank], axis=0)
    spread = conv_back(scaled, a_high, a_low) * pass_b[COLS:-COLS, :]
    straight = incoming * pass_b[own, :]
    return folded(
        jnp.concatenate(
            [
                column_sum(grad_out),
                column_sum(grad_out * norm_a[own, :]),
                column_sum(spread) + column_sum(straight),
                column_sum(spread * norm_b[COLS:-COLS, :])
                + column_sum(straight * norm_b[own, :]),
            ],
            axis=0,
        )
    )


def first_kernel(main, pass_a, norm_a, pass_b, norm_b, params, a_high, a_low, sums):
    parts = first_sums(main, pass_a, norm_a, pass_b, norm_b, params, a_high, a_low)
    sums[...] = jnp.broadcast_to(parts[None], sums.shape)


def opening_kernel(share, main, pass_a, norm_a, pass_b, norm_b, params, a_high, a_low, sums):
    parts = first_sums(main, pass_a, norm_a, pass_b, norm_b, params, a_high, a_low)
    parts = jnp.concatenate([parts, jnp.sum(share[...], axis=0)], axis=0)
    sums[...] = jnp.broadcast_to(parts[None], sums.shape)


def second_kernel(
    count, tiles, step, flags, received, exchanged, top, main, bottom, pass_a, norm_a, pass_b, norm_b,
    params, a_high, a_low, b_high, b_low, old_act, old_grad, old_gain,
    out, out_head, out_tail, act, grad, gain,
):
    incoming = jnp.concatenate([top[...], main[...], bottom[...]], axis=0)
    gamma_a, inverse_a, gamma_b, inverse_b = (params[i : i + 1, :] for i in range(4))
    totals = jnp.sum(received[:, :8, :], axis=0)
    totals = jnp.concatenate([totals[:4], totals[4:]], axis=1)
    response = exchanged[:, 8:, :].reshape(GROUPS, 8, C // 2)
    flat, full = (
        jnp.concatenate([response[:, start + chunk, :] for chunk in range(4)], axis=1)
        for start in (0, 4)
    )
    groups, spread = group_matrix(), spread_matrix()
    means_a = dot(totals[0:2] * gamma_a, groups, highest) * (1.0 / count)
    shift = dot(means_a[0:1], flat, highest) + dot(means_a[1:2], full, highest)
    totals_b = totals[2:4] - jnp.concatenate([shift[:, :C], shift[:, C:]], axis=0)
    means_b = dot(totals_b * gamma_b, groups, highest) * (1.0 / count)
    wide_a = dot(means_a, spread, highest)
    wide_b = dot(means_b, spread, highest)
    inside = inside_rows(flags, tiles)
    grad_a = inverse_a * (
        incoming * pass_a[...] * gamma_a - inside * wide_a[0:1] - norm_a[...] * wide_a[1:2]
    )
    middle = incoming[COLS:-COLS] + conv_back(grad_a, a_high, a_low)
    grad_b = inverse_b * (
        middle * pass_b[COLS:-COLS, :] * gamma_b
        - inside[COLS:-COLS] * wide_b[0:1]
        - norm_b[COLS:-COLS, :] * wide_b[1:2]
    )
    last = middle[COLS:-COLS] + conv_back(grad_b, b_high, b_low)
    out[...] = last
    out_head[...] = last[: 2 * COLS]
    out_tail[...] = last[-2 * COLS :]
    active = flags[0] == step
    upper = flags[1] == 1
    act[...] = jnp.where(
        active, jnp.where(upper, middle[COLS:-COLS], last), old_act[...]
    )
    grad[...] = jnp.where(
        active, jnp.where(upper, grad_a[2 * COLS : -2 * COLS], grad_b[COLS:-COLS]), old_grad[...]
    )
    pair_a = jnp.concatenate([totals[1:2], totals[0:1]], axis=0)
    pair_b = jnp.concatenate([totals_b[1:2], totals_b[0:1]], axis=0)
    gain[...] = jnp.where(active, jnp.where(upper, pair_a, pair_b), old_gain[...])


def kernel_grad_kernel(tiles, flags, top, main, bottom, grad, mine, other):
    share = C // tiles
    image = jnp.concatenate([top[...], main[...], bottom[...]], axis=0)
    turned = grad[...].T.reshape(tiles // 2, 2, share, OWN)
    even = turned[:, 0].reshape(C // 2, OWN)
    odd = turned[:, 1].reshape(C // 2, OWN)
    core = flags[3]
    left = split(
        jnp.concatenate(
            [jnp.where(core == 0, even, odd), jnp.where(core == 0, odd, even)], axis=0
        )
    )
    for col_tap in range(3):
        high, low = split(shifted(image, col_tap - 1))
        for row_tap in range(3):
            start = (row_tap + 2) * COLS
            product = dot3(left, (high[start : start + OWN], low[start : start + OWN]))
            where = slice((row_tap * 3 + col_tap) * C, (row_tap * 3 + col_tap + 1) * C)
            mine[:, where] = product[: C // 2]
            other[:, where] = product[C // 2 :]


def call(body, out_shape, operands, flagged, **options):
    spec = pl.BlockSpec(memory_space=pltpu.VMEM)
    in_specs = [spec] * len(operands)
    if flagged:
        in_specs[0] = pl.BlockSpec(memory_space=pltpu.SMEM)
    many = isinstance(out_shape, tuple)
    return pl.pallas_call(
        body,
        out_shape=out_shape,
        in_specs=in_specs,
        out_specs=tuple(spec for _ in out_shape) if many else spec,
        compiler_params=pltpu.CompilerParams(vmem_limit_bytes=40 * 2**20),
        **options,
    )(*operands)


def shape(*dims, dtype=f32):
    return jax.ShapeDtypeStruct(dims, dtype)


def prepare(tiles, count, flags, kernel, near, far, gathered, fields, partner_fields):
    tap = lambda rows: pl.BlockSpec((1, rows, C), lambda i: (i, 0, 0))
    whole = lambda *dims: pl.BlockSpec(dims, lambda i: (0,) * len(dims))
    tall = 12 * COLS
    return pl.pallas_call(
        functools.partial(prepare_kernel, tiles, count),
        grid=(9,),
        out_shape=tuple(shape(9, C, C, dtype=bf16) for _ in range(4))
        + tuple(shape(tall, C) for _ in range(4))
        + (shape(8, C), shape(GROUPS, 8, C // 2)),
        in_specs=[
            pl.BlockSpec(memory_space=pltpu.SMEM),
            tap(C),
            tap(C // 2),
            tap(C // 2),
            whole(*gathered.shape),
            whole(*fields.shape),
            whole(*fields.shape),
        ],
        out_specs=tuple(tap(C) for _ in range(4))
        + tuple(whole(tall, C) for _ in range(4))
        + (whole(8, C), whole(GROUPS, 8, C // 2)),
        scratch_shapes=[
            pltpu.VMEM((2 * C, OWN), bf16),
            pltpu.VMEM((2 * C, OWN), bf16),
            pltpu.VMEM((3, tall, C + C // 2), f32),
            pltpu.VMEM((2 * C, C), f32),
            pltpu.VMEM((2 * C, C), f32),
        ],
        compiler_params=pltpu.CompilerParams(vmem_limit_bytes=40 * 2**20),
    )(flags, kernel, near, far, gathered, fields, partner_fields)


def on_device(acts, kernels, gammas, pass_mask, drop_mask, path_mask, cotangent):
    pairs = lax.axis_size("pair")
    tiles = lax.axis_size(TILE)
    devices = 2 * pairs * tiles
    pair, member, core = (lax.axis_index(a) for a in ("pair", "member", "core"))
    tile = lax.axis_index(TILE)
    count = tiles * OWN * (C // GROUPS)
    swap = [(0, 1), (1, 0)]

    own_kernel = kernels[0].reshape(9, C, C)
    half = lax.dynamic_slice_in_dim(own_kernel, core * (C // 2), C // 2, axis=1)
    near = lax.ppermute(half, "member", swap)

    passing = (
        pass_mask[0, 0].astype(f32)
        * (drop_mask[0, 0].astype(f32)[..., None] / keep_drop)
        * (path_mask[0].astype(f32)[:, None, None] / keep_path)
    ).reshape(OWN, C)
    image = acts[0, 0].reshape(OWN, C)
    start = cotangent[0].reshape(OWN, C)

    def neighbours(value, step, jump):
        return lax.ppermute(
            value,
            ALL,
            [
                (i, i - jump * 2 * tiles + step)
                for i in range(jump * 2 * tiles, devices)
                if 0 <= i % tiles + step < tiles
            ],
        )

    from_above = neighbours(
        jnp.concatenate([image[-3 * COLS :], passing[-2 * COLS :], start[-2 * COLS :]]), 1, 0
    )
    from_below = neighbours(
        jnp.concatenate([image[: 3 * COLS], passing[: 2 * COLS], start[: 2 * COLS]]), -1, 0
    )
    cuts = (0, 3 * COLS, 5 * COLS, 7 * COLS)
    above = [from_above[a:b] for a, b in zip(cuts, cuts[1:])]
    below = [from_below[a:b] for a, b in zip(cuts, cuts[1:])]
    image_parts = (above[0], image, below[0])
    passing = jnp.concatenate([above[1], passing, below[1]])
    tall = 12 * COLS
    conv_out, sums = call(
        forward_kernel,
        (shape(tall, C), shape(2 * tiles, 8, C // 2)),
        image_parts + (own_kernel, gammas),
        False,
    )
    fields = jnp.stack([conv_out, passing])
    partner_fields = lax.ppermute(fields, "member", swap)
    near, sums = lax.optimization_barrier((near, sums))
    far = lax.ppermute(near, "core", swap)
    far, partner_fields, sums = lax.optimization_barrier((far, partner_fields, sums))
    gathered = lax.all_to_all(sums, ("member",) + TILE, 0, 0)
    flags = jnp.stack([pairs - 1 - pair, member, tile, core]).astype(jnp.int32)
    prepared = prepare(
        tiles, count, flags, own_kernel, near, far, gathered, fields, partner_fields
    )
    a_high, a_low, b_high, b_low = (w.reshape(3, 3 * C, C) for w in prepared[:4])
    masks, params, response = prepared[4:8], prepared[8], prepared[9]
    piece = GROUPS // tiles
    response = lax.all_to_all(response.reshape(tiles, piece * 8, C // 2), TILE, 0, 0)

    top, main, bottom = above[2], start, below[2]
    act = jnp.zeros((OWN, C), f32)
    grad = jnp.zeros((OWN, C), f32)
    gain = jnp.zeros((2, C), f32)
    exchanged = None
    for step in range(pairs):
        shared = masks + (params, a_high, a_low)
        if step == 0:
            sums = call(
                opening_kernel,
                shape(tiles, 8 + piece * 8, C // 2),
                (response, main) + shared,
                False,
            )
            received = exchanged = lax.all_to_all(sums, TILE, 0, 0)
        else:
            sums = call(first_kernel, shape(tiles, 8, C // 2), (main,) + shared, False)
            sums, top, bottom = lax.optimization_barrier((sums, top, bottom))
            received = lax.all_to_all(sums, TILE, 0, 0)
        main, head, tail, act, grad, gain = call(
            functools.partial(second_kernel, count, tiles, step),
            (
                shape(OWN, C),
                shape(2 * COLS, C),
                shape(2 * COLS, C),
                shape(OWN, C),
                shape(OWN, C),
                shape(2, C),
            ),
            (flags, received, exchanged, top, main, bottom)
            + shared
            + (b_high, b_low, act, grad, gain),
            True,
        )
        if step < pairs - 1:
            main, top, bottom = (
                neighbours(main, 0, 1),
                neighbours(tail, 1, 1),
                neighbours(head, -1, 1),
            )

    mine, other = call(
        functools.partial(kernel_grad_kernel, tiles),
        (shape(C // 2, 9 * C), shape(C // 2, 9 * C)),
        (flags,) + image_parts + (grad,),
        True,
    )
    share = C // tiles
    mine = mine + lax.ppermute(other, "core", swap)
    for axis in ("x", "z"):
        parts = lax.axis_size(axis)
        mine = jnp.sum(
            lax.all_to_all(mine.reshape(parts, mine.shape[0] // parts, 9 * C), axis, 0, 0), axis=0
        )
    kernel_share = jnp.transpose(mine.reshape(share, 3, 3, C), (1, 2, 3, 0))
    return (
        act.reshape(1, 1, ROWS, COLS, C),
        kernel_share[None],
        gain[None],
    )


def solution(mesh):
    sections, tiles = mesh.shape["section"], mesh.shape["tile"]
    across = 4 if tiles == 32 else 1
    finer = Mesh(
        mesh.devices.reshape(sections // 2, 2, tiles // (2 * across), across, 2), ALL
    )
    return jax.shard_map(
        on_device,
        mesh=finer,
        in_specs=(
            P(SECTION, None, TILE, None, None),
            P(SECTION, None, None, None, None),
            P(SECTION, None),
            P(SECTION, None, TILE, None, None),
            P(SECTION, None, TILE, None),
            P(SECTION, None),
            P(None, TILE, None, None),
        ),
        out_specs=(
            P(SECTION, None, TILE, None, None),
            P(SECTION, None, None, None, TILE),
            P(SECTION, None, None),
        ),
        check_vma=False,
    )
```

```python
import functools

import jax
import jax.numpy as jnp
from jax import lax
from jax.experimental import pallas as pl
from jax.experimental.pallas import tpu as pltpu
from jax.sharding import Mesh
from jax.sharding import PartitionSpec as P

GROUPS = 32
C = 256
COLS = 16
ROWS = 8
OWN = ROWS * COLS

keep_drop = 0.9
keep_path = 0.75
eps = 1e-05
highest = lax.Precision.HIGHEST
f32 = jnp.float32
bf16 = jnp.bfloat16

SECTION = ("pair", "member")
TILE = ("x", "z", "core")
ALL = SECTION + TILE


def split(values):
    high = values.astype(bf16)
    return high, (values - high.astype(f32)).astype(bf16)


def dot(left, right, precision=None):
    return jnp.dot(left, right, preferred_element_type=f32, precision=precision)


def dot3(left, right):
    lh, ll = left
    rh, rl = right
    return dot(lh, rh) + dot(ll, rh) + dot(lh, rl)


def shifted(values, offset):
    if offset == 0:
        return values
    count = values.shape[0]
    column = lax.broadcasted_iota(jnp.int32, values.shape, 0) & (COLS - 1)
    rolled = pltpu.roll(values, (-offset) % count, 0)
    edge = COLS - 1 if offset > 0 else 0
    return jnp.where(column == edge, 0.0, rolled)


def conv_back(field, high_ref, low_ref):
    wide = jnp.concatenate([shifted(field, 1), field, shifted(field, -1)], axis=1)
    high, low = split(wide)
    count = field.shape[0] - 2 * COLS
    total = None
    for tap in range(3):
        start = (2 - tap) * COLS
        part = dot3(
            (high[start : start + count], low[start : start + count]),
            (high_ref[tap], low_ref[tap]),
        )
        total = part if total is None else total + part
    return total


def group_matrix(width=GROUPS, first=0):
    channel = lax.broadcasted_iota(jnp.int32, (C, width), 0)
    group = lax.broadcasted_iota(jnp.int32, (C, width), 1)
    return jnp.where((channel >> 3) + first == group, 1.0, 0.0).astype(f32)


def spread_matrix(width=GROUPS, first=0):
    channel = lax.broadcasted_iota(jnp.int32, (width, C), 1)
    group = lax.broadcasted_iota(jnp.int32, (width, C), 0)
    return jnp.where((channel >> 3) + first == group, 1.0, 0.0).astype(f32)


def column_sum(values):
    return jnp.sum(values, axis=0, keepdims=True)


def forward_kernel(above, main, below, passing, start, kernel, gamma, fields, sums):
    image = jnp.concatenate([above[: 3 * COLS, :], main[...], below[: 3 * COLS, :]], axis=0)
    count = tall = image.shape[0] - 2 * COLS
    total = None
    for col_tap in range(3):
        high, low = split(shifted(image, col_tap - 1))
        for row_tap in range(3):
            start_row = row_tap * COLS
            part = dot3(
                (high[start_row : start_row + count], low[start_row : start_row + count]),
                split(kernel[row_tap * 3 + col_tap]),
            )
            total = part if total is None else total + part
    fields[:tall, :] = total
    fields[tall : 2 * tall, :] = jnp.concatenate(
        [above[3 * COLS : 5 * COLS, :], passing[...], below[3 * COLS : 5 * COLS, :]], axis=0
    )
    fields[2 * tall :, :] = jnp.concatenate([gamma[...], jnp.zeros((7, C), f32)], axis=0)
    own = total[2 * COLS : 2 * COLS + OWN]
    grad_out = start[...] * passing[...]
    half = C // 2
    straight, weighted = column_sum(grad_out), column_sum(grad_out * own)
    block = jnp.concatenate(
        [
            dot(column_sum(own), group_matrix(half), highest)
            + dot(column_sum(own * own), group_matrix(half, GROUPS), highest),
            straight[:, :half],
            straight[:, half:],
            weighted[:, :half],
            weighted[:, half:],
            jnp.zeros((3, half), f32),
        ],
        axis=0,
    )
    sums[...] = jnp.broadcast_to(block[None], sums.shape)


def prepare_kernel(
    tiles, count, flags, own, near, near_two, far, far_two, gathered, fields, partner_fields,
    a_high, a_low, b_high, b_low, pass_a, norm_a, pass_b, norm_b, params, opening, response,
    high_scr, low_scr, field_scr, flat_scr, full_scr,
):
    tap = pl.program_id(0)
    core = flags[3]
    member = flags[1]

    @pl.when(tap == 0)
    def _():
        stats = jnp.sum(gathered[...].reshape(2, tiles, 8, C // 2), axis=1)
        half = C // 2
        inside = inside_rows(flags, tiles)
        tall = 12 * COLS

        def section(which, conv_out, passing, gamma, pass_ref, norm_ref, row):
            grouped = stats[which, 0:1] * (1.0 / count)
            mean = dot(grouped, spread_matrix(half), highest)
            square = dot(grouped, spread_matrix(half, GROUPS), highest)
            inverse = lax.rsqrt(square - mean * mean + eps)
            pass_ref[...] = passing
            norm_ref[...] = (conv_out - mean) * inverse * inside
            params[row : row + 1, :] = gamma
            params[row + 1 : row + 2, :] = inverse
            if which == 1:
                block = stats[which]
                straight = jnp.concatenate([block[1:2], block[2:3]], axis=1)
                weighted = jnp.concatenate([block[3:4], block[4:5]], axis=1)
                opening[0:1, :] = straight
                opening[1:2, :] = inverse * (weighted - mean * straight)

        upper = member == 1
        mine, other = fields[:tall, :], partner_fields[:tall, :]
        my_pass, other_pass = fields[tall : 2 * tall, :], partner_fields[tall : 2 * tall, :]
        my_gamma = fields[2 * tall : 2 * tall + 1, :]
        other_gamma = partner_fields[2 * tall : 2 * tall + 1, :]
        section(1, jnp.where(upper, mine, other), jnp.where(upper, my_pass, other_pass),
                jnp.where(upper, my_gamma, other_gamma), pass_a, norm_a, 0)
        section(0, jnp.where(upper, other, mine), jnp.where(upper, other_pass, my_pass),
                jnp.where(upper, other_gamma, my_gamma), pass_b, norm_b, 2)
        params[4:8, :] = jnp.zeros((4, C), f32)
        passing = pass_b[2 * COLS : 2 * COLS + OWN]
        normed = norm_b[2 * COLS : 2 * COLS + OWN]
        high, low = split(jnp.concatenate([passing.T, (passing * normed).T], axis=0))
        high_scr[...] = high
        low_scr[...] = low
        both = jnp.concatenate([norm_a[...], inside[:, : C // 2]], axis=1)
        field_scr[0] = shifted(both, 1)
        field_scr[1] = both
        field_scr[2] = shifted(both, -1)
        flat_scr[...] = jnp.zeros_like(flat_scr)
        full_scr[...] = jnp.zeros_like(full_scr)

    near_tap = jnp.concatenate([near[0], near_two[0]], axis=0)
    far_tap = jnp.concatenate([far[0], far_two[0]], axis=0)
    partner = jnp.concatenate(
        [jnp.where(core == 0, near_tap, far_tap), jnp.where(core == 0, far_tap, near_tap)], axis=0
    )
    kernel_a = jnp.where(member == 1, own[0], partner)
    kernel_b = jnp.where(member == 1, partner, own[0])
    high, low = split(kernel_a.T)
    a_high[0] = high
    a_low[0] = low
    high, low = split(kernel_b.T)
    b_high[0] = high
    b_low[0] = low

    row_tap = tap // 3
    col_tap = tap - row_tap * 3
    begin = pl.multiple_of((3 - row_tap) * COLS, COLS)
    moved = split(field_scr[col_tap, pl.ds(begin, OWN), :])
    moment = dot3((high_scr[...], low_scr[...]), moved)
    full_scr[:C, :] += moment[:C, :C] * kernel_a
    full_scr[C:, :] += moment[C:, :C] * kernel_a
    flat_scr[:C, :] += moment[:C, C : C + 1] * kernel_a
    flat_scr[C:, :] += moment[C:, C : C + 1] * kernel_a

    @pl.when(tap == 8)
    def _():
        groups = group_matrix()
        contract = (((0,), (1,)), ((), ()))
        for index, scratch in enumerate((flat_scr, full_scr)):
            part = lax.dot_general(
                groups, scratch[...] * params[1:2, :], contract,
                preferred_element_type=f32, precision=highest,
            )
            for chunk in range(4):
                response[:, index * 4 + chunk, :] = part[:, chunk * 128 : (chunk + 1) * 128]


def inside_rows(flags, tiles):
    row = lax.broadcasted_iota(jnp.int32, (12 * COLS, C), 0)
    first = jnp.where(flags[2] == 0, 2 * COLS, 0)
    last = jnp.where(flags[2] == tiles - 1, 10 * COLS, 12 * COLS)
    return jnp.where((row >= first) & (row < last), 1.0, 0.0).astype(f32)


def folded(values):
    return jnp.concatenate([values[:, : C // 2], values[:, C // 2 :]], axis=0)


def first_sums(main, pass_a, norm_a, pass_b, norm_b, params, a_high, a_low):
    own = slice(2 * COLS, 2 * COLS + OWN)
    incoming = main[...]
    grad_out = incoming * pass_a[own, :]
    blank = jnp.zeros((2 * COLS, C), f32)
    scaled = jnp.concatenate([blank, grad_out * (params[0:1, :] * params[1:2, :]), blank], axis=0)
    spread = conv_back(scaled, a_high, a_low) * pass_b[COLS:-COLS, :]
    straight = incoming * pass_b[own, :]
    return folded(
        jnp.concatenate(
            [
                column_sum(grad_out),
                column_sum(grad_out * norm_a[own, :]),
                column_sum(spread) + column_sum(straight),
                column_sum(spread * norm_b[COLS:-COLS, :])
                + column_sum(straight * norm_b[own, :]),
            ],
            axis=0,
        )
    )


def first_kernel(main, pass_a, norm_a, pass_b, norm_b, params, a_high, a_low, sums):
    parts = first_sums(main, pass_a, norm_a, pass_b, norm_b, params, a_high, a_low)
    sums[...] = jnp.broadcast_to(parts[None], sums.shape)


def sharing_kernel(share, main, pass_a, norm_a, pass_b, norm_b, params, a_high, a_low, sums):
    parts = first_sums(main, pass_a, norm_a, pass_b, norm_b, params, a_high, a_low)
    parts = jnp.concatenate([parts, share[...]], axis=0)
    sums[...] = jnp.broadcast_to(parts[None], sums.shape)


def group_means(totals, gamma, count):
    return dot(totals * gamma, group_matrix(), highest) * (1.0 / count)


def through(incoming, passing, normed, inside, gamma, inverse, means, high, low):
    wide = dot(means, spread_matrix(), highest)
    grad = inverse * (incoming * passing * gamma - inside * wide[0:1] - normed * wide[1:2])
    return grad, incoming[COLS:-COLS] + conv_back(grad, high, low)


def gain_rows(totals):
    return jnp.concatenate([totals[1:2], totals[0:1]], axis=0)


def opening_kernel(
    count, tiles, flags, opening, above, main, below, response, pass_a, norm_a, pass_b, norm_b,
    params, a_high, a_low, sums, middle, grad_a,
):
    incoming = jnp.concatenate(
        [above[5 * COLS :, :], main[...], below[5 * COLS :, :]], axis=0
    )
    means = group_means(opening[...], params[0:1, :], count)
    grad, passed = through(
        incoming, pass_a[...], norm_a[...], inside_rows(flags, tiles),
        params[0:1, :], params[1:2, :], means, a_high, a_low,
    )
    middle[...] = passed
    grad_a[...] = grad[2 * COLS : -2 * COLS]
    own = slice(2 * COLS, 2 * COLS + OWN)
    grad_b = passed[COLS:-COLS] * pass_b[own, :]
    parts = folded(
        jnp.concatenate(
            [
                jnp.zeros((2, C), f32),
                column_sum(grad_b),
                column_sum(grad_b * norm_b[own, :]),
            ],
            axis=0,
        )
    )
    sums[...] = jnp.concatenate(
        [jnp.broadcast_to(parts[None], (tiles, 8, C // 2)), response[...]], axis=1
    )


def closing_kernel(
    count, tiles, flags, received, opening, middle, grad_a, pass_b, norm_b, params, b_high, b_low,
    out, out_head, out_tail, act, grad, gain, share,
):
    totals = jnp.sum(received[...], axis=0)
    share[...] = totals[8:]
    totals = jnp.concatenate([totals[:4], totals[4:8]], axis=1)[2:4]
    means = group_means(totals, params[2:3, :], count)
    near = middle[...]
    grad_b, last = through(
        near, pass_b[COLS:-COLS, :], norm_b[COLS:-COLS, :],
        inside_rows(flags, tiles)[COLS:-COLS], params[2:3, :], params[3:4, :],
        means, b_high, b_low,
    )
    out[...] = last
    out_head[...] = last[: 2 * COLS]
    out_tail[...] = last[-2 * COLS :]
    active = flags[0] == 0
    upper = flags[1] == 1
    act[...] = jnp.where(active, jnp.where(upper, near[COLS:-COLS], last), 0.0)
    grad[...] = jnp.where(active, jnp.where(upper, grad_a[...], grad_b[COLS:-COLS]), 0.0)
    gain[...] = jnp.where(
        active, jnp.where(upper, gain_rows(opening[...]), gain_rows(totals)), 0.0
    )


def second_kernel(
    count, tiles, step, flags, received, exchanged, top, main, bottom, pass_a, norm_a, pass_b, norm_b,
    params, a_high, a_low, b_high, b_low, old_act, old_grad, old_gain,
    out, out_head, out_tail, act, grad, gain,
):
    incoming = jnp.concatenate([top[...], main[...], bottom[...]], axis=0)
    totals = jnp.sum(received[:, :8, :], axis=0)
    totals = jnp.concatenate([totals[:4], totals[4:]], axis=1)
    response = exchanged[:, 8:, :].reshape(GROUPS, 8, C // 2)
    flat, full = (
        jnp.concatenate([response[:, start + chunk, :] for chunk in range(4)], axis=1)
        for start in (0, 4)
    )
    inside = inside_rows(flags, tiles)
    means_a = group_means(totals[0:2], params[0:1, :], count)
    shift = dot(means_a[0:1], flat, highest) + dot(means_a[1:2], full, highest)
    totals_b = totals[2:4] - jnp.concatenate([shift[:, :C], shift[:, C:]], axis=0)
    means_b = group_means(totals_b, params[2:3, :], count)
    grad_a, middle = through(
        incoming, pass_a[...], norm_a[...], inside, params[0:1, :], params[1:2, :],
        means_a, a_high, a_low,
    )
    grad_b, last = through(
        middle, pass_b[COLS:-COLS, :], norm_b[COLS:-COLS, :], inside[COLS:-COLS],
        params[2:3, :], params[3:4, :], means_b, b_high, b_low,
    )
    out[...] = last
    out_head[...] = last[: 2 * COLS]
    out_tail[...] = last[-2 * COLS :]
    active = flags[0] == step
    upper = flags[1] == 1
    act[...] = jnp.where(active, jnp.where(upper, middle[COLS:-COLS], last), old_act[...])
    grad[...] = jnp.where(
        active, jnp.where(upper, grad_a[2 * COLS : -2 * COLS], grad_b[COLS:-COLS]), old_grad[...]
    )
    gain[...] = jnp.where(
        active, jnp.where(upper, gain_rows(totals[0:2]), gain_rows(totals_b)), old_gain[...]
    )


def kernel_grad_kernel(tiles, flags, above, main, below, grad, mine, other):
    share = C // tiles
    image = jnp.concatenate([above[: 3 * COLS, :], main[...], below[: 3 * COLS, :]], axis=0)
    turned = grad[...].T.reshape(tiles // 2, 2, share, OWN)
    even = turned[:, 0].reshape(C // 2, OWN)
    odd = turned[:, 1].reshape(C // 2, OWN)
    core = flags[3]
    left = split(
        jnp.concatenate(
            [jnp.where(core == 0, even, odd), jnp.where(core == 0, odd, even)], axis=0
        )
    )
    for col_tap in range(3):
        high, low = split(shifted(image, col_tap - 1))
        for row_tap in range(3):
            start = (row_tap + 2) * COLS
            product = dot3(left, (high[start : start + OWN], low[start : start + OWN]))
            where = slice((row_tap * 3 + col_tap) * C, (row_tap * 3 + col_tap + 1) * C)
            mine[:, where] = product[: C // 2]
            other[:, where] = product[C // 2 :]


def call(body, out_shape, operands, flagged, **options):
    spec = pl.BlockSpec(memory_space=pltpu.VMEM)
    in_specs = [spec] * len(operands)
    if flagged:
        in_specs[0] = pl.BlockSpec(memory_space=pltpu.SMEM)
    many = isinstance(out_shape, tuple)
    return pl.pallas_call(
        body,
        out_shape=out_shape,
        in_specs=in_specs,
        out_specs=tuple(spec for _ in out_shape) if many else spec,
        compiler_params=pltpu.CompilerParams(vmem_limit_bytes=40 * 2**20),
        **options,
    )(*operands)


def shape(*dims, dtype=f32):
    return jax.ShapeDtypeStruct(dims, dtype)


def prepare(tiles, count, flags, kernel, pieces, gathered, fields, partner_fields):
    tap = lambda rows: pl.BlockSpec((1, rows, C), lambda i: (i, 0, 0))
    whole = lambda *dims: pl.BlockSpec(dims, lambda i: (0,) * len(dims))
    tall = 12 * COLS
    return pl.pallas_call(
        functools.partial(prepare_kernel, tiles, count),
        grid=(9,),
        out_shape=tuple(shape(9, C, C, dtype=bf16) for _ in range(4))
        + tuple(shape(tall, C) for _ in range(4))
        + (shape(8, C), shape(2, C), shape(GROUPS, 8, C // 2)),
        in_specs=[
            pl.BlockSpec(memory_space=pltpu.SMEM),
            tap(C),
            *(tap(C // 4) for _ in range(4)),
            whole(*gathered.shape),
            whole(*fields.shape),
            whole(*fields.shape),
        ],
        out_specs=tuple(tap(C) for _ in range(4))
        + tuple(whole(tall, C) for _ in range(4))
        + (whole(8, C), whole(2, C), whole(GROUPS, 8, C // 2)),
        scratch_shapes=[
            pltpu.VMEM((2 * C, OWN), bf16),
            pltpu.VMEM((2 * C, OWN), bf16),
            pltpu.VMEM((3, tall, C + C // 2), f32),
            pltpu.VMEM((2 * C, C), f32),
            pltpu.VMEM((2 * C, C), f32),
        ],
        compiler_params=pltpu.CompilerParams(vmem_limit_bytes=40 * 2**20),
    )(flags, kernel, *pieces, gathered, fields, partner_fields)


def on_device(acts, kernels, gammas, pass_mask, drop_mask, path_mask, cotangent):
    pairs = lax.axis_size("pair")
    tiles = lax.axis_size(TILE)
    devices = 2 * pairs * tiles
    pair, member, core = (lax.axis_index(a) for a in ("pair", "member", "core"))
    tile = lax.axis_index(TILE)
    count = tiles * OWN * (C // GROUPS)
    swap = [(0, 1), (1, 0)]

    own_kernel = kernels[0].reshape(9, C, C)
    quarters = [
        lax.dynamic_slice_in_dim(own_kernel, core * (C // 2) + q * (C // 4), C // 4, axis=1)
        for q in range(2)
    ]
    layers = lax.axis_size("z")
    route = [(i, layers + i) for i in range(layers)] + [(layers + i, i) for i in range(layers)]
    route_two = [(i, layers + (i - 1) % layers) for i in range(layers)] + [
        (layers + (i - 1) % layers, i) for i in range(layers)
    ]
    near = lax.ppermute(quarters[0], ("member", "z"), route)
    near_two = lax.ppermute(quarters[1], ("member", "z"), route_two)
    flags = jnp.stack([pairs - 1 - pair, member, tile, core]).astype(jnp.int32)
    acts, pass_mask, cotangent, flags, *quarters = lax.optimization_barrier(
        (acts, pass_mask, cotangent, flags, *quarters)
    )

    passing = (
        pass_mask[0, 0].astype(f32)
        * (drop_mask[0, 0].astype(f32)[..., None] / keep_drop)
        * (path_mask[0].astype(f32)[:, None, None] / keep_path)
    ).reshape(OWN, C)
    image = acts[0, 0].reshape(OWN, C)
    start = cotangent[0].reshape(OWN, C)

    def neighbours(value, step, source=None):
        size = 2 * tiles
        first, last, jump = (0, devices, 0) if source is None else (
            source * size, (source + 1) * size, size,
        )
        return lax.ppermute(
            value,
            ALL,
            [
                (i, i - jump + step)
                for i in range(first, last)
                if 0 <= i % tiles + step < tiles
            ],
        )

    from_above = neighbours(
        jnp.concatenate([image[-3 * COLS :], passing[-2 * COLS :], start[-2 * COLS :]]), 1
    )
    from_below = neighbours(
        jnp.concatenate([image[: 3 * COLS], passing[: 2 * COLS], start[: 2 * COLS]]), -1
    )
    tall = 12 * COLS
    edges = (from_above, image, from_below)
    fields, sums = call(
        forward_kernel,
        (shape(2 * tall + 8, C), shape(2 * tiles, 8, C // 2)),
        edges + (passing, start, own_kernel, gammas),
        False,
    )
    partner_fields = lax.ppermute(fields, "member", swap)
    near, near_two, partner_fields, sums = lax.optimization_barrier(
        (near, near_two, partner_fields, sums)
    )
    far = lax.ppermute(near, "core", swap)
    far_two = lax.ppermute(near_two, "core", swap)
    far, far_two, sums = lax.optimization_barrier((far, far_two, sums))
    gathered = lax.all_to_all(sums, ("member",) + TILE, 0, 0)
    prepared = prepare(
        tiles, count, flags, own_kernel, (near, near_two, far, far_two), gathered, fields,
        partner_fields,
    )
    a_high, a_low, b_high, b_low = (w.reshape(3, 3 * C, C) for w in prepared[:4])
    masks, params, opening, response = prepared[4:8], prepared[8], prepared[9], prepared[10]
    piece = GROUPS // tiles
    block = 8 + piece * 8
    response = response.reshape(tiles, piece * 8, C // 2)
    shared = masks + (params, a_high, a_low)
    rows_out = (
        shape(OWN, C),
        shape(2 * COLS, C),
        shape(2 * COLS, C),
        shape(OWN, C),
        shape(OWN, C),
        shape(2, C),
    )

    sums, middle, grad_a = call(
        functools.partial(opening_kernel, count, tiles),
        (shape(tiles, block, C // 2), shape(OWN + 2 * COLS, C), shape(OWN, C)),
        (flags, opening, from_above, start, from_below, response) + shared,
        True,
    )
    received = lax.all_to_all(sums, TILE, 0, 0)
    main, head, tail, act, grad, gain, share = call(
        functools.partial(closing_kernel, count, tiles),
        rows_out + (shape(piece * 8, C // 2),),
        (flags, received, opening, middle, grad_a) + masks[2:] + (params, b_high, b_low),
        True,
    )
    exchanged = None
    for step in range(1, pairs):
        main, top, bottom = (
            neighbours(main, 0, pairs - step),
            neighbours(tail, 1, pairs - step),
            neighbours(head, -1, pairs - step),
        )
        if step == 1:
            sums = call(sharing_kernel, shape(tiles, block, C // 2), (share, main) + shared, False)
        else:
            sums = call(first_kernel, shape(tiles, 8, C // 2), (main,) + shared, False)
        sums, top, bottom = lax.optimization_barrier((sums, top, bottom))
        received = lax.all_to_all(sums, TILE, 0, 0)
        if step == 1:
            exchanged = received
        main, head, tail, act, grad, gain = call(
            functools.partial(second_kernel, count, tiles, step),
            rows_out,
            (flags, received, exchanged, top, main, bottom)
            + shared
            + (b_high, b_low, act, grad, gain),
            True,
        )

    mine, other = call(
        functools.partial(kernel_grad_kernel, tiles),
        (shape(C // 2, 9 * C), shape(C // 2, 9 * C)),
        (flags,) + edges + (grad,),
        True,
    )
    share = C // tiles
    mine = mine + lax.ppermute(other, "core", swap)
    for axis in ("x", "z"):
        parts = lax.axis_size(axis)
        mine = jnp.sum(
            lax.all_to_all(mine.reshape(parts, mine.shape[0] // parts, 9 * C), axis, 0, 0), axis=0
        )
    kernel_share = jnp.transpose(mine.reshape(share, 3, 3, C), (1, 2, 3, 0))
    return (
        act.reshape(1, 1, ROWS, COLS, C),
        kernel_share[None],
        gain[None],
    )


def solution(mesh):
    sections, tiles = mesh.shape["section"], mesh.shape["tile"]
    across = min(4, tiles // 2)
    finer = Mesh(
        mesh.devices.reshape(sections // 2, 2, tiles // (2 * across), across, 2), ALL
    )
    return jax.shard_map(
        on_device,
        mesh=finer,
        in_specs=(
            P(SECTION, None, TILE, None, None),
            P(SECTION, None, None, None, None),
            P(SECTION, None),
            P(SECTION, None, TILE, None, None),
            P(SECTION, None, TILE, None),
            P(SECTION, None),
            P(None, TILE, None, None),
        ),
        out_specs=(
            P(SECTION, None, TILE, None, None),
            P(SECTION, None, None, None, TILE),
            P(SECTION, None, None),
        ),
        check_vma=False,
    )
```

```python
import functools

import jax
import jax.numpy as jnp
from jax import lax
from jax.experimental import pallas as pl
from jax.experimental.pallas import tpu as pltpu
from jax.sharding import Mesh
from jax.sharding import PartitionSpec as P

GROUPS = 32
C = 256
COLS = 16
ROWS = 8
OWN = ROWS * COLS
LANES = 4 * GROUPS

keep_drop = 0.9
keep_path = 0.75
eps = 1e-05
highest = lax.Precision.HIGHEST
f32 = jnp.float32
bf16 = jnp.bfloat16

SECTION = ("pair", "member")
TILE = ("x", "z", "core")
ALL = SECTION + TILE


def split(values):
    high = values.astype(bf16)
    return high, (values - high.astype(f32)).astype(bf16)


def dot(left, right, precision=None):
    return jnp.dot(left, right, preferred_element_type=f32, precision=precision)


def dot3(left, right):
    lh, ll = left
    rh, rl = right
    return dot(lh, rh) + dot(ll, rh) + dot(lh, rl)


def shifted(values, offset):
    if offset == 0:
        return values
    count = values.shape[0]
    column = lax.broadcasted_iota(jnp.int32, values.shape, 0) & (COLS - 1)
    rolled = pltpu.roll(values, (-offset) % count, 0)
    edge = COLS - 1 if offset > 0 else 0
    return jnp.where(column == edge, 0.0, rolled)


def conv_back(field, high_ref, low_ref):
    wide = jnp.concatenate([shifted(field, 1), field, shifted(field, -1)], axis=1)
    high, low = split(wide)
    count = field.shape[0] - 2 * COLS
    total = None
    for tap in range(3):
        start = (2 - tap) * COLS
        part = dot3(
            (high[start : start + count], low[start : start + count]),
            (high_ref[tap], low_ref[tap]),
        )
        total = part if total is None else total + part
    return total


def group_matrix(width=GROUPS, first=0):
    channel = lax.broadcasted_iota(jnp.int32, (C, width), 0)
    group = lax.broadcasted_iota(jnp.int32, (C, width), 1)
    return jnp.where((channel >> 3) + first == group, 1.0, 0.0).astype(f32)


def exact_dot(left, right):
    count = left.shape[0]
    high = left.astype(bf16)
    rest = left - high.astype(f32)
    middle = rest.astype(bf16)
    low = (rest - middle.astype(f32)).astype(bf16)
    pieces = jnp.concatenate([x.astype(f32) for x in (high, middle, low)], axis=0).astype(bf16)
    product = dot(pieces, right.astype(bf16))
    return product[:count] + product[count : 2 * count] + product[2 * count :]


def lane_quarter(rows):
    return lax.broadcasted_iota(jnp.int32, (rows, LANES), 1) >> 5


def repeated_groups():
    channel = lax.broadcasted_iota(jnp.int32, (C, LANES), 0)
    lane = lax.broadcasted_iota(jnp.int32, (C, LANES), 1)
    return jnp.where((channel >> 3) == (lane & (GROUPS - 1)), 1.0, 0.0)


def pack(rows):
    sums = exact_dot(rows, repeated_groups())
    row = lax.broadcasted_iota(jnp.int32, (4, LANES), 0)
    return column_sum(jnp.where(lane_quarter(4) == row, sums, 0.0))


def unpack(packed):
    row = lax.broadcasted_iota(jnp.int32, (4, LANES), 0)
    apart = jnp.where(lane_quarter(4) == row, jnp.broadcast_to(packed, (4, LANES)), 0.0)
    lane = lax.broadcasted_iota(jnp.int32, (LANES, C), 0)
    channel = lax.broadcasted_iota(jnp.int32, (LANES, C), 1)
    return exact_dot(apart, jnp.where((channel >> 3) == (lane & (GROUPS - 1)), 1.0, 0.0))


def column_sum(values):
    return jnp.sum(values, axis=0, keepdims=True)


def edge_kernel(path, image, mask, drop, start, passing, tail, head):
    pixel = lax.broadcasted_iota(jnp.int32, (OWN, ROWS), 0)
    row = lax.broadcasted_iota(jnp.int32, (OWN, ROWS), 1)
    by_row = dot(
        jnp.where((pixel >> 4) == row, 1.0, 0.0).astype(bf16), drop[...].astype(f32).astype(bf16)
    )
    pixel = lax.broadcasted_iota(jnp.int32, (OWN, COLS), 0)
    column = lax.broadcasted_iota(jnp.int32, (OWN, COLS), 1)
    kept = jnp.sum(jnp.where((pixel & (COLS - 1)) == column, by_row, 0.0), axis=1, keepdims=True)
    kept_path = path[0, 0].astype(f32) / keep_path
    values = mask[...].astype(f32) * (kept / keep_drop) * kept_path
    passing[...] = values
    tail[: 3 * COLS, :] = image[-3 * COLS :, :]
    tail[3 * COLS : 5 * COLS, :] = values[-2 * COLS :]
    tail[5 * COLS :, :] = start[-2 * COLS :, :]
    head[: 3 * COLS, :] = image[: 3 * COLS, :]
    head[3 * COLS : 5 * COLS, :] = values[: 2 * COLS]
    head[5 * COLS :, :] = start[: 2 * COLS, :]


def forward_kernel(above, main, below, passing, start, kernel, gamma, fields, sums):
    image = jnp.concatenate([above[: 3 * COLS, :], main[...], below[: 3 * COLS, :]], axis=0)
    count = tall = image.shape[0] - 2 * COLS
    total = None
    for col_tap in range(3):
        high, low = split(shifted(image, col_tap - 1))
        for row_tap in range(3):
            start_row = row_tap * COLS
            part = dot3(
                (high[start_row : start_row + count], low[start_row : start_row + count]),
                split(kernel[row_tap * 3 + col_tap]),
            )
            total = part if total is None else total + part
    fields[:tall, :] = total
    fields[tall : 2 * tall, :] = jnp.concatenate(
        [above[3 * COLS : 5 * COLS, :], passing[...], below[3 * COLS : 5 * COLS, :]], axis=0
    )
    fields[2 * tall :, :] = jnp.concatenate([gamma[...], jnp.zeros((7, C), f32)], axis=0)
    own = total[2 * COLS : 2 * COLS + OWN]
    grad_out = start[...] * passing[...]
    packed = pack(
        jnp.concatenate(
            [
                column_sum(own),
                column_sum(own * own),
                column_sum(grad_out) * gamma[...],
                column_sum(grad_out * own) * gamma[...],
            ],
            axis=0,
        )
    )
    sums[...] = jnp.broadcast_to(packed[None], sums.shape)


def prepare_kernel(
    tiles, count, flags, own, near, near_two, far, far_two, gathered, fields, partner_fields,
    a_high, a_low, b_high, b_low, pass_a, norm_a, pass_b, norm_b, params, opening, response,
    high_scr, low_scr, field_scr, flat_scr, full_scr,
):
    tap = pl.program_id(0)
    core = flags[3]
    member = flags[1]

    @pl.when(tap == 0)
    def _():
        stats = [
            jnp.sum(gathered[which * tiles : (which + 1) * tiles], axis=0) * (1.0 / count)
            for which in range(2)
        ]
        inside = inside_rows(flags, tiles)
        tall = 12 * COLS

        def section(which, conv_out, passing, gamma, pass_ref, norm_ref, row):
            wide = unpack(stats[which])
            mean, square = wide[0:1], wide[1:2]
            inverse = lax.rsqrt(square - mean * mean + eps)
            pass_ref[...] = passing
            norm_ref[...] = (conv_out - mean) * inverse * inside
            params[row : row + 1, :] = gamma
            params[row + 1 : row + 2, :] = inverse
            if which == 1:
                opening[0:1, :] = wide[2:3]
                opening[1:2, :] = inverse * (wide[3:4] - mean * wide[2:3])

        upper = member == 1
        mine, other = fields[:tall, :], partner_fields[:tall, :]
        my_pass, other_pass = fields[tall : 2 * tall, :], partner_fields[tall : 2 * tall, :]
        my_gamma = fields[2 * tall : 2 * tall + 1, :]
        other_gamma = partner_fields[2 * tall : 2 * tall + 1, :]
        section(1, jnp.where(upper, mine, other), jnp.where(upper, my_pass, other_pass),
                jnp.where(upper, my_gamma, other_gamma), pass_a, norm_a, 0)
        section(0, jnp.where(upper, other, mine), jnp.where(upper, other_pass, my_pass),
                jnp.where(upper, other_gamma, my_gamma), pass_b, norm_b, 2)
        params[4:8, :] = jnp.zeros((4, C), f32)
        passing = pass_b[2 * COLS : 2 * COLS + OWN]
        normed = norm_b[2 * COLS : 2 * COLS + OWN]
        high, low = split(jnp.concatenate([passing.T, (passing * normed).T], axis=0))
        high_scr[...] = high
        low_scr[...] = low
        both = jnp.concatenate([norm_a[...], inside[:, : C // 2]], axis=1)
        field_scr[0] = shifted(both, 1)
        field_scr[1] = both
        field_scr[2] = shifted(both, -1)
        flat_scr[...] = jnp.zeros_like(flat_scr)
        full_scr[...] = jnp.zeros_like(full_scr)

    near_tap = jnp.concatenate([near[0], near_two[0]], axis=0)
    far_tap = jnp.concatenate([far[0], far_two[0]], axis=0)
    partner = jnp.concatenate(
        [jnp.where(core == 0, near_tap, far_tap), jnp.where(core == 0, far_tap, near_tap)], axis=0
    )
    kernel_a = jnp.where(member == 1, own[0], partner)
    kernel_b = jnp.where(member == 1, partner, own[0])
    high, low = split(kernel_a.T)
    a_high[0] = high
    a_low[0] = low
    high, low = split(kernel_b.T)
    b_high[0] = high
    b_low[0] = low

    row_tap = tap // 3
    col_tap = tap - row_tap * 3
    begin = pl.multiple_of((3 - row_tap) * COLS, COLS)
    moved = split(field_scr[col_tap, pl.ds(begin, OWN), :])
    moment = dot3((high_scr[...], low_scr[...]), moved)
    full_scr[:C, :] += moment[:C, :C] * kernel_a
    full_scr[C:, :] += moment[C:, :C] * kernel_a
    flat_scr[:C, :] += moment[:C, C : C + 1] * kernel_a
    flat_scr[C:, :] += moment[C:, C : C + 1] * kernel_a

    @pl.when(tap == 8)
    def _():
        groups = group_matrix()
        contract = (((0,), (1,)), ((), ()))
        total = jnp.zeros((GROUPS, LANES), f32)
        for index, scratch in enumerate((flat_scr, full_scr)):
            part = lax.dot_general(
                groups, scratch[...] * params[1:2, :], contract,
                preferred_element_type=f32, precision=highest,
            )
            for side in range(2):
                sums = exact_dot(
                    part[:, side * C : (side + 1) * C] * params[2:3, :], repeated_groups()
                )
                total += jnp.where(lane_quarter(GROUPS) == index * 2 + side, sums, 0.0)
        response[...] = total * (1.0 / count)


def inside_rows(flags, tiles):
    row = lax.broadcasted_iota(jnp.int32, (12 * COLS, C), 0)
    first = jnp.where(flags[2] == 0, 2 * COLS, 0)
    last = jnp.where(flags[2] == tiles - 1, 10 * COLS, 12 * COLS)
    return jnp.where((row >= first) & (row < last), 1.0, 0.0).astype(f32)


def first_sums(main, pass_a, norm_a, pass_b, norm_b, params, a_high, a_low):
    own = slice(2 * COLS, 2 * COLS + OWN)
    incoming = main[...]
    grad_out = incoming * pass_a[own, :]
    blank = jnp.zeros((2 * COLS, C), f32)
    scaled = jnp.concatenate([blank, grad_out * (params[0:1, :] * params[1:2, :]), blank], axis=0)
    spread = conv_back(scaled, a_high, a_low) * pass_b[COLS:-COLS, :]
    straight = incoming * pass_b[own, :]
    gamma_a, gamma_b = params[0:1, :], params[2:3, :]
    return pack(
        jnp.concatenate(
            [
                column_sum(grad_out) * gamma_a,
                column_sum(grad_out * norm_a[own, :]) * gamma_a,
                (column_sum(spread) + column_sum(straight)) * gamma_b,
                (
                    column_sum(spread * norm_b[COLS:-COLS, :])
                    + column_sum(straight * norm_b[own, :])
                )
                * gamma_b,
            ],
            axis=0,
        )
    )


def first_kernel(main, pass_a, norm_a, pass_b, norm_b, params, a_high, a_low, sums):
    parts = first_sums(main, pass_a, norm_a, pass_b, norm_b, params, a_high, a_low)
    sums[...] = jnp.broadcast_to(parts[None], sums.shape)


def sharing_kernel(share, main, pass_a, norm_a, pass_b, norm_b, params, a_high, a_low, sums):
    parts = first_sums(main, pass_a, norm_a, pass_b, norm_b, params, a_high, a_low)
    parts = jnp.concatenate([parts, share[...]], axis=0)
    sums[...] = jnp.broadcast_to(parts[None], sums.shape)


def through(incoming, passing, normed, inside, gamma, inverse, means, high, low):
    grad = inverse * (incoming * passing * gamma - inside * means[0:1] - normed * means[1:2])
    return grad, incoming[COLS:-COLS] + conv_back(grad, high, low)


def gain_sums(grad_out, normed):
    return jnp.concatenate([column_sum(grad_out * normed), column_sum(grad_out)], axis=0)


def opening_kernel(
    tiles, flags, opening, above, main, below, response, pass_a, norm_a, pass_b, norm_b,
    params, a_high, a_low, sums, middle, grad_a, gain_a,
):
    incoming = jnp.concatenate(
        [above[5 * COLS :, :], main[...], below[5 * COLS :, :]], axis=0
    )
    grad, passed = through(
        incoming, pass_a[...], norm_a[...], inside_rows(flags, tiles),
        params[0:1, :], params[1:2, :], opening[...], a_high, a_low,
    )
    middle[...] = passed
    grad_a[...] = grad[2 * COLS : -2 * COLS]
    own = slice(2 * COLS, 2 * COLS + OWN)
    gain_a[...] = gain_sums(main[...] * pass_a[own, :], norm_a[own, :])
    grad_b = passed[COLS:-COLS] * pass_b[own, :]
    gamma_b = params[2:3, :]
    packed = pack(
        jnp.concatenate(
            [
                jnp.zeros((2, C), f32),
                column_sum(grad_b) * gamma_b,
                column_sum(grad_b * norm_b[own, :]) * gamma_b,
            ],
            axis=0,
        )
    )
    sums[:, 0:1, :] = jnp.broadcast_to(packed[None], (tiles, 1, LANES))
    if tiles == GROUPS:
        sums[:, 1, :] = response[...]
    else:
        sums[:, 1:, :] = response[...].reshape(tiles, GROUPS // tiles, LANES)


def closing_kernel(
    count, tiles, flags, received, middle, grad_a, gain_a, pass_b, norm_b, params, b_high, b_low,
    out, out_head, out_tail, act, grad, gain, share,
):
    share[...] = jnp.sum(received[:, 1:, :], axis=0)
    means = unpack(jnp.sum(received[:, 0:1, :], axis=0) * (1.0 / count))[2:4]
    near = middle[...]
    grad_b, last = through(
        near, pass_b[COLS:-COLS, :], norm_b[COLS:-COLS, :],
        inside_rows(flags, tiles)[COLS:-COLS], params[2:3, :], params[3:4, :],
        means, b_high, b_low,
    )
    out[...] = last
    out_head[...] = last[: 2 * COLS]
    out_tail[...] = last[-2 * COLS :]
    active = flags[0] == 0
    upper = flags[1] == 1
    own = slice(2 * COLS, 2 * COLS + OWN)
    gain_b = gain_sums(near[COLS:-COLS] * pass_b[own, :], norm_b[own, :])
    act[...] = jnp.where(active, jnp.where(upper, near[COLS:-COLS], last), 0.0)
    grad[...] = jnp.where(active, jnp.where(upper, grad_a[...], grad_b[COLS:-COLS]), 0.0)
    gain[...] = jnp.where(active, jnp.where(upper, gain_a[...], gain_b), 0.0)


def second_kernel(
    count, tiles, step, flags, received, exchanged, top, main, bottom, pass_a, norm_a, pass_b, norm_b,
    params, a_high, a_low, b_high, b_low, old_act, old_grad, old_gain,
    out, out_head, out_tail, act, grad, gain,
):
    incoming = jnp.concatenate([top[...], main[...], bottom[...]], axis=0)
    means = jnp.sum(received[:, 0:1, :], axis=0) * (1.0 / count)
    if tiles == GROUPS:
        response = exchanged[:, 1, :]
    else:
        response = exchanged[:, 1:, :].reshape(GROUPS, LANES)
    right = lane_quarter(GROUPS) >= 2
    response = jnp.concatenate(
        [
            jnp.where(right, pltpu.roll(response, 2 * GROUPS, 1), 0.0),
            jnp.where(right, response, 0.0),
            jnp.zeros((2 * GROUPS, LANES), f32),
        ],
        axis=0,
    )
    means_a = unpack(means)[0:2]
    means_b = unpack(means - dot(means, response, highest))[2:4]
    inside = inside_rows(flags, tiles)
    grad_a, middle = through(
        incoming, pass_a[...], norm_a[...], inside, params[0:1, :], params[1:2, :],
        means_a, a_high, a_low,
    )
    grad_b, last = through(
        middle, pass_b[COLS:-COLS, :], norm_b[COLS:-COLS, :], inside[COLS:-COLS],
        params[2:3, :], params[3:4, :], means_b, b_high, b_low,
    )
    out[...] = last
    out_head[...] = last[: 2 * COLS]
    out_tail[...] = last[-2 * COLS :]
    active = flags[0] == step
    upper = flags[1] == 1
    own = slice(2 * COLS, 2 * COLS + OWN)
    gain_a = gain_sums(main[...] * pass_a[own, :], norm_a[own, :])
    gain_b = gain_sums(middle[COLS:-COLS] * pass_b[own, :], norm_b[own, :])
    act[...] = jnp.where(active, jnp.where(upper, middle[COLS:-COLS], last), old_act[...])
    grad[...] = jnp.where(
        active, jnp.where(upper, grad_a[2 * COLS : -2 * COLS], grad_b[COLS:-COLS]), old_grad[...]
    )
    gain[...] = jnp.where(active, jnp.where(upper, gain_a, gain_b), old_gain[...])


def kernel_grad_kernel(tiles, flags, above, main, below, grad, gain, mine, other):
    share = C // tiles
    image = jnp.concatenate([above[: 3 * COLS, :], main[...], below[: 3 * COLS, :]], axis=0)
    turned = grad[...].T.reshape(tiles // 2, 2, share, OWN)
    even = turned[:, 0].reshape(C // 2, OWN)
    odd = turned[:, 1].reshape(C // 2, OWN)
    core = flags[3]
    left = split(
        jnp.concatenate(
            [jnp.where(core == 0, even, odd), jnp.where(core == 0, odd, even)], axis=0
        )
    )
    for col_tap in range(3):
        high, low = split(shifted(image, col_tap - 1))
        for row_tap in range(3):
            start = (row_tap + 2) * COLS
            product = dot3(left, (high[start : start + OWN], low[start : start + OWN]))
            where = slice((row_tap * 3 + col_tap) * C, (row_tap * 3 + col_tap + 1) * C)
            mine[:, where] = product[: C // 2]
            other[:, where] = product[C // 2 :]
    half = C // 2
    eight = jnp.concatenate([gain[:, :half], gain[:, half:], jnp.zeros((4, half), f32)], axis=0)
    copies = jnp.broadcast_to(eight[None], (half // 8, 8, half)).reshape(half, half)
    mine[:, 9 * C :] = copies
    other[:, 9 * C :] = copies


def call(body, out_shape, operands, flagged, **options):
    spec = pl.BlockSpec(memory_space=pltpu.VMEM)
    in_specs = [spec] * len(operands)
    if flagged:
        in_specs[0] = pl.BlockSpec(memory_space=pltpu.SMEM)
    many = isinstance(out_shape, tuple)
    return pl.pallas_call(
        body,
        out_shape=out_shape,
        in_specs=in_specs,
        out_specs=tuple(spec for _ in out_shape) if many else spec,
        compiler_params=pltpu.CompilerParams(vmem_limit_bytes=40 * 2**20),
        **options,
    )(*operands)


def shape(*dims, dtype=f32):
    return jax.ShapeDtypeStruct(dims, dtype)


def prepare(tiles, count, flags, kernel, pieces, gathered, fields, partner_fields):
    tap = lambda rows: pl.BlockSpec((1, rows, C), lambda i: (i, 0, 0))
    whole = lambda *dims: pl.BlockSpec(dims, lambda i: (0,) * len(dims))
    tall = 12 * COLS
    return pl.pallas_call(
        functools.partial(prepare_kernel, tiles, count),
        grid=(9,),
        out_shape=tuple(shape(9, C, C, dtype=bf16) for _ in range(4))
        + tuple(shape(tall, C) for _ in range(4))
        + (shape(8, C), shape(2, C), shape(GROUPS, LANES)),
        in_specs=[
            pl.BlockSpec(memory_space=pltpu.SMEM),
            tap(C),
            *(tap(C // 4) for _ in range(4)),
            whole(*gathered.shape),
            whole(*fields.shape),
            whole(*fields.shape),
        ],
        out_specs=tuple(tap(C) for _ in range(4))
        + tuple(whole(tall, C) for _ in range(4))
        + (whole(8, C), whole(2, C), whole(GROUPS, LANES)),
        scratch_shapes=[
            pltpu.VMEM((2 * C, OWN), bf16),
            pltpu.VMEM((2 * C, OWN), bf16),
            pltpu.VMEM((3, tall, C + C // 2), f32),
            pltpu.VMEM((2 * C, C), f32),
            pltpu.VMEM((2 * C, C), f32),
        ],
        compiler_params=pltpu.CompilerParams(vmem_limit_bytes=40 * 2**20),
    )(flags, kernel, *pieces, gathered, fields, partner_fields)


def on_device(acts, kernels, gammas, pass_mask, drop_mask, path_mask, cotangent):
    pairs = lax.axis_size("pair")
    tiles = lax.axis_size(TILE)
    devices = 2 * pairs * tiles
    pair, member, core = (lax.axis_index(a) for a in ("pair", "member", "core"))
    tile = lax.axis_index(TILE)
    count = tiles * OWN * (C // GROUPS)
    swap = [(0, 1), (1, 0)]

    own_kernel = kernels[0].reshape(9, C, C)
    quarters = [
        lax.dynamic_slice_in_dim(own_kernel, core * (C // 2) + q * (C // 4), C // 4, axis=1)
        for q in range(2)
    ]
    layers = lax.axis_size("z")
    route = [(i, layers + i) for i in range(layers)] + [(layers + i, i) for i in range(layers)]
    route_two = [(i, layers + (i - 1) % layers) for i in range(layers)] + [
        (layers + (i - 1) % layers, i) for i in range(layers)
    ]
    near = lax.ppermute(quarters[0], ("member", "z"), route)
    near_two = lax.ppermute(quarters[1], ("member", "z"), route_two)
    flags = jnp.stack([pairs - 1 - pair, member, tile, core]).astype(jnp.int32)
    acts, pass_mask, drop_mask, cotangent, flags, *quarters = lax.optimization_barrier(
        (acts, pass_mask, drop_mask, cotangent, flags, *quarters)
    )

    image = acts[0, 0].reshape(OWN, C)
    start = cotangent[0].reshape(OWN, C)
    passing, tail, head = call(
        edge_kernel,
        (shape(OWN, C), shape(7 * COLS, C), shape(7 * COLS, C)),
        (path_mask, image, pass_mask[0, 0].reshape(OWN, C), drop_mask[0, 0], start),
        True,
    )

    def neighbours(value, step, source=None):
        size = 2 * tiles
        first, last, jump = (0, devices, 0) if source is None else (
            source * size, (source + 1) * size, size,
        )
        return lax.ppermute(
            value,
            ALL,
            [
                (i, i - jump + step)
                for i in range(first, last)
                if 0 <= i % tiles + step < tiles
            ],
        )

    from_above = neighbours(tail, 1)
    from_below = neighbours(head, -1)
    tall = 12 * COLS
    edges = (from_above, image, from_below)
    fields, sums = call(
        forward_kernel,
        (shape(2 * tall + 8, C), shape(2 * tiles, 1, LANES)),
        edges + (passing, start, own_kernel, gammas),
        False,
    )
    partner_fields = lax.ppermute(fields, "member", swap)
    gathered = lax.all_to_all(sums, ("member",) + TILE, 0, 0)
    near, near_two, gathered = lax.optimization_barrier((near, near_two, gathered))
    far = lax.ppermute(near, "core", swap)
    far_two = lax.ppermute(near_two, "core", swap)
    prepared = prepare(
        tiles, count, flags, own_kernel, (near, near_two, far, far_two), gathered, fields,
        partner_fields,
    )
    a_high, a_low, b_high, b_low = (w.reshape(3, 3 * C, C) for w in prepared[:4])
    masks, params, opening, response = prepared[4:8], prepared[8], prepared[9], prepared[10]
    piece = GROUPS // tiles
    block = 1 + piece
    shared = masks + (params, a_high, a_low)
    rows_out = (
        shape(OWN, C),
        shape(2 * COLS, C),
        shape(2 * COLS, C),
        shape(OWN, C),
        shape(OWN, C),
        shape(2, C),
    )

    sums, middle, grad_a, gain_a = call(
        functools.partial(opening_kernel, tiles),
        (shape(tiles, block, LANES), shape(OWN + 2 * COLS, C), shape(OWN, C), shape(2, C)),
        (flags, opening, from_above, start, from_below, response) + shared,
        True,
    )
    received = lax.all_to_all(sums, TILE, 0, 0)
    main, head, tail, act, grad, gain, share = call(
        functools.partial(closing_kernel, count, tiles),
        rows_out + (shape(piece, LANES),),
        (flags, received, middle, grad_a, gain_a) + masks[2:] + (params, b_high, b_low),
        True,
    )
    exchanged = None
    for step in range(1, pairs):
        main, top, bottom = (
            neighbours(main, 0, pairs - step),
            neighbours(tail, 1, pairs - step),
            neighbours(head, -1, pairs - step),
        )
        if step == 1:
            sums = call(sharing_kernel, shape(tiles, block, LANES), (share, main) + shared, False)
        else:
            sums = call(first_kernel, shape(tiles, 1, LANES), (main,) + shared, False)
        sums, top, bottom = lax.optimization_barrier((sums, top, bottom))
        received = lax.all_to_all(sums, TILE, 0, 0)
        if step == 1:
            exchanged = received
        main, head, tail, act, grad, gain = call(
            functools.partial(second_kernel, count, tiles, step),
            rows_out,
            (flags, received, exchanged, top, main, bottom)
            + shared
            + (b_high, b_low, act, grad, gain),
            True,
        )

    width = 9 * C + C // 2
    mine, other = call(
        functools.partial(kernel_grad_kernel, tiles),
        (shape(C // 2, width), shape(C // 2, width)),
        (flags,) + edges + (grad, gain),
        True,
    )
    mine = mine + lax.ppermute(other, "core", swap)
    for axis in ("x", "z"):
        parts = lax.axis_size(axis)
        mine = jnp.sum(
            lax.all_to_all(mine.reshape(parts, mine.shape[0] // parts, width), axis, 0, 0), axis=0
        )
    kernel_share = jnp.transpose(mine[:, : 9 * C].reshape(C // tiles, 3, 3, C), (1, 2, 3, 0))
    gain = jnp.concatenate([mine[0:2, 9 * C :], mine[2:4, 9 * C :]], axis=1)
    return (
        act.reshape(1, 1, ROWS, COLS, C),
        kernel_share[None],
        gain[None],
    )


def solution(mesh):
    sections, tiles = mesh.shape["section"], mesh.shape["tile"]
    across = min(4, tiles // 2)
    finer = Mesh(
        mesh.devices.reshape(sections // 2, 2, tiles // (2 * across), across, 2), ALL
    )
    return jax.shard_map(
        on_device,
        mesh=finer,
        in_specs=(
            P(SECTION, None, TILE, None, None),
            P(SECTION, None, None, None, None),
            P(SECTION, None),
            P(SECTION, None, TILE, None, None),
            P(SECTION, None, TILE, None),
            P(SECTION, None),
            P(None, TILE, None, None),
        ),
        out_specs=(
            P(SECTION, None, TILE, None, None),
            P(SECTION, None, None, None, TILE),
            P(SECTION, None, None),
        ),
        check_vma=False,
    )
```

```python
import functools

import jax
import jax.numpy as jnp
from jax import lax
from jax.experimental import pallas as pl
from jax.experimental.pallas import tpu as pltpu
from jax.sharding import Mesh
from jax.sharding import PartitionSpec as P

GROUPS = 32
C = 256
COLS = 16
ROWS = 8
OWN = ROWS * COLS
LANES = 4 * GROUPS

keep_drop = 0.9
keep_path = 0.75
eps = 1e-05
highest = lax.Precision.HIGHEST
f32 = jnp.float32
bf16 = jnp.bfloat16

SECTION = ("pair", "member")
TILE = ("x", "z", "core")
ALL = SECTION + TILE


def split(values):
    high = values.astype(bf16)
    return high, (values - high.astype(f32)).astype(bf16)


def dot(left, right, precision=None):
    return jnp.dot(left, right, preferred_element_type=f32, precision=precision)


def dot3(left, right):
    lh, ll = left
    rh, rl = right
    return dot(lh, rh) + dot(ll, rh) + dot(lh, rl)


def shifted(values, offset):
    if offset == 0:
        return values
    count = values.shape[0]
    column = lax.broadcasted_iota(jnp.int32, values.shape, 0) & (COLS - 1)
    rolled = pltpu.roll(values, (-offset) % count, 0)
    edge = COLS - 1 if offset > 0 else 0
    return jnp.where(column == edge, 0.0, rolled)


def conv_back(field, high_ref, low_ref):
    wide = jnp.concatenate([shifted(field, 1), field, shifted(field, -1)], axis=1)
    high, low = split(wide)
    count = field.shape[0] - 2 * COLS
    total = None
    for tap in range(3):
        start = (2 - tap) * COLS
        part = dot3(
            (high[start : start + count], low[start : start + count]),
            (high_ref[tap], low_ref[tap]),
        )
        total = part if total is None else total + part
    return total


def group_matrix(width=GROUPS, first=0):
    channel = lax.broadcasted_iota(jnp.int32, (C, width), 0)
    group = lax.broadcasted_iota(jnp.int32, (C, width), 1)
    return jnp.where((channel >> 3) + first == group, 1.0, 0.0).astype(f32)


def exact_dot(left, right):
    count = left.shape[0]
    high = left.astype(bf16)
    rest = left - high.astype(f32)
    middle = rest.astype(bf16)
    low = (rest - middle.astype(f32)).astype(bf16)
    pieces = jnp.concatenate([x.astype(f32) for x in (high, middle, low)], axis=0).astype(bf16)
    product = dot(pieces, right.astype(bf16))
    return product[:count] + product[count : 2 * count] + product[2 * count :]


def lane_quarter(rows):
    return lax.broadcasted_iota(jnp.int32, (rows, LANES), 1) >> 5


def repeated_groups():
    channel = lax.broadcasted_iota(jnp.int32, (C, LANES), 0)
    lane = lax.broadcasted_iota(jnp.int32, (C, LANES), 1)
    return jnp.where((channel >> 3) == (lane & (GROUPS - 1)), 1.0, 0.0)


def pack(rows):
    sums = exact_dot(rows, repeated_groups())
    row = lax.broadcasted_iota(jnp.int32, (4, LANES), 0)
    return column_sum(jnp.where(lane_quarter(4) == row, sums, 0.0))


def unpack(packed):
    row = lax.broadcasted_iota(jnp.int32, (4, LANES), 0)
    apart = jnp.where(lane_quarter(4) == row, jnp.broadcast_to(packed, (4, LANES)), 0.0)
    lane = lax.broadcasted_iota(jnp.int32, (LANES, C), 0)
    channel = lax.broadcasted_iota(jnp.int32, (LANES, C), 1)
    return exact_dot(apart, jnp.where((channel >> 3) == (lane & (GROUPS - 1)), 1.0, 0.0))


def column_sum(values):
    return jnp.sum(values, axis=0, keepdims=True)


def edge_kernel(path, image, mask, drop, start, passing, tail, head):
    pixel = lax.broadcasted_iota(jnp.int32, (OWN, ROWS), 0)
    row = lax.broadcasted_iota(jnp.int32, (OWN, ROWS), 1)
    by_row = dot(
        jnp.where((pixel >> 4) == row, 1.0, 0.0).astype(bf16), drop[...].astype(f32).astype(bf16)
    )
    pixel = lax.broadcasted_iota(jnp.int32, (OWN, COLS), 0)
    column = lax.broadcasted_iota(jnp.int32, (OWN, COLS), 1)
    kept = jnp.sum(jnp.where((pixel & (COLS - 1)) == column, by_row, 0.0), axis=1, keepdims=True)
    kept_path = path[0, 0].astype(f32) / keep_path
    values = mask[...].astype(f32) * (kept / keep_drop) * kept_path
    passing[...] = values
    tail[: 3 * COLS, :] = image[-3 * COLS :, :]
    tail[3 * COLS : 5 * COLS, :] = values[-2 * COLS :]
    tail[5 * COLS :, :] = start[-2 * COLS :, :]
    head[: 3 * COLS, :] = image[: 3 * COLS, :]
    head[3 * COLS : 5 * COLS, :] = values[: 2 * COLS]
    head[5 * COLS :, :] = start[: 2 * COLS, :]


def forward_kernel(above, main, below, passing, start, kernel, gamma, fields, sums):
    image = jnp.concatenate([above[: 3 * COLS, :], main[...], below[: 3 * COLS, :]], axis=0)
    count = tall = image.shape[0] - 2 * COLS
    total = None
    for col_tap in range(3):
        high, low = split(shifted(image, col_tap - 1))
        for row_tap in range(3):
            start_row = row_tap * COLS
            part = dot3(
                (high[start_row : start_row + count], low[start_row : start_row + count]),
                split(kernel[row_tap * 3 + col_tap]),
            )
            total = part if total is None else total + part
    fields[:tall, :] = total
    fields[tall : 2 * tall, :] = jnp.concatenate(
        [above[3 * COLS : 5 * COLS, :], passing[...], below[3 * COLS : 5 * COLS, :]], axis=0
    )
    fields[2 * tall :, :] = jnp.concatenate([gamma[...], jnp.zeros((7, C), f32)], axis=0)
    own = total[2 * COLS : 2 * COLS + OWN]
    grad_out = start[...] * passing[...]
    packed = pack(
        jnp.concatenate(
            [
                column_sum(own),
                column_sum(own * own),
                column_sum(grad_out) * gamma[...],
                column_sum(grad_out * own) * gamma[...],
            ],
            axis=0,
        )
    )
    sums[...] = jnp.broadcast_to(packed[None], sums.shape)


def prepare_kernel(
    tiles, count, flags, own, near, near_two, far, far_two, gathered, fields, partner_fields,
    a_high, a_low, b_high, b_low, pass_a, norm_a, pass_b, norm_b, params, opening, response,
    high_scr, low_scr, field_scr, flat_scr, full_scr,
):
    tap = pl.program_id(0)
    core = flags[3]
    member = flags[1]

    @pl.when(tap == 0)
    def _():
        stats = [
            jnp.sum(gathered[which * tiles : (which + 1) * tiles], axis=0) * (1.0 / count)
            for which in range(2)
        ]
        inside = inside_rows(flags, tiles)
        tall = 12 * COLS

        def section(which, conv_out, passing, gamma, pass_ref, norm_ref, row):
            wide = unpack(stats[which])
            mean, square = wide[0:1], wide[1:2]
            inverse = lax.rsqrt(square - mean * mean + eps)
            pass_ref[...] = passing
            norm_ref[...] = (conv_out - mean) * inverse * inside
            params[row : row + 1, :] = gamma
            params[row + 1 : row + 2, :] = inverse
            if which == 1:
                opening[0:1, :] = wide[2:3]
                opening[1:2, :] = inverse * (wide[3:4] - mean * wide[2:3])

        upper = member == 1
        mine, other = fields[:tall, :], partner_fields[:tall, :]
        my_pass, other_pass = fields[tall : 2 * tall, :], partner_fields[tall : 2 * tall, :]
        my_gamma = fields[2 * tall : 2 * tall + 1, :]
        other_gamma = partner_fields[2 * tall : 2 * tall + 1, :]
        section(1, jnp.where(upper, mine, other), jnp.where(upper, my_pass, other_pass),
                jnp.where(upper, my_gamma, other_gamma), pass_a, norm_a, 0)
        section(0, jnp.where(upper, other, mine), jnp.where(upper, other_pass, my_pass),
                jnp.where(upper, other_gamma, my_gamma), pass_b, norm_b, 2)
        params[4:8, :] = jnp.zeros((4, C), f32)
        passing = pass_b[2 * COLS : 2 * COLS + OWN]
        normed = norm_b[2 * COLS : 2 * COLS + OWN]
        high, low = split(jnp.concatenate([passing.T, (passing * normed).T], axis=0))
        high_scr[...] = high
        low_scr[...] = low
        both = jnp.concatenate([norm_a[...], inside[:, : C // 2]], axis=1)
        field_scr[0] = shifted(both, 1)
        field_scr[1] = both
        field_scr[2] = shifted(both, -1)
        flat_scr[...] = jnp.zeros_like(flat_scr)
        full_scr[...] = jnp.zeros_like(full_scr)

    near_tap = jnp.concatenate([near[0], near_two[0]], axis=0)
    far_tap = jnp.concatenate([far[0], far_two[0]], axis=0)
    partner = jnp.concatenate(
        [jnp.where(core == 0, near_tap, far_tap), jnp.where(core == 0, far_tap, near_tap)], axis=0
    )
    kernel_a = jnp.where(member == 1, own[0], partner)
    kernel_b = jnp.where(member == 1, partner, own[0])
    high, low = split(kernel_a.T)
    a_high[0] = high
    a_low[0] = low
    high, low = split(kernel_b.T)
    b_high[0] = high
    b_low[0] = low

    row_tap = tap // 3
    col_tap = tap - row_tap * 3
    begin = pl.multiple_of((3 - row_tap) * COLS, COLS)
    moved = split(field_scr[col_tap, pl.ds(begin, OWN), :])
    moment = dot3((high_scr[...], low_scr[...]), moved)
    full_scr[:C, :] += moment[:C, :C] * kernel_a
    full_scr[C:, :] += moment[C:, :C] * kernel_a
    flat_scr[:C, :] += moment[:C, C : C + 1] * kernel_a
    flat_scr[C:, :] += moment[C:, C : C + 1] * kernel_a

    @pl.when(tap == 8)
    def _():
        groups = group_matrix()
        contract = (((0,), (1,)), ((), ()))
        total = jnp.zeros((GROUPS, LANES), f32)
        for index, scratch in enumerate((flat_scr, full_scr)):
            part = lax.dot_general(
                groups, scratch[...] * params[1:2, :], contract,
                preferred_element_type=f32, precision=highest,
            )
            for side in range(2):
                sums = exact_dot(
                    part[:, side * C : (side + 1) * C] * params[2:3, :], repeated_groups()
                )
                total += jnp.where(lane_quarter(GROUPS) == index * 2 + side, sums, 0.0)
        response[...] = total * (1.0 / count)


def inside_rows(flags, tiles):
    row = lax.broadcasted_iota(jnp.int32, (12 * COLS, C), 0)
    first = jnp.where(flags[2] == 0, 2 * COLS, 0)
    last = jnp.where(flags[2] == tiles - 1, 10 * COLS, 12 * COLS)
    return jnp.where((row >= first) & (row < last), 1.0, 0.0).astype(f32)


def first_sums(main, pass_a, norm_a, pass_b, norm_b, params, a_high, a_low):
    own = slice(2 * COLS, 2 * COLS + OWN)
    incoming = main[...]
    grad_out = incoming * pass_a[own, :]
    blank = jnp.zeros((2 * COLS, C), f32)
    scaled = jnp.concatenate([blank, grad_out * (params[0:1, :] * params[1:2, :]), blank], axis=0)
    spread = conv_back(scaled, a_high, a_low) * pass_b[COLS:-COLS, :]
    straight = incoming * pass_b[own, :]
    gamma_a, gamma_b = params[0:1, :], params[2:3, :]
    return pack(
        jnp.concatenate(
            [
                column_sum(grad_out) * gamma_a,
                column_sum(grad_out * norm_a[own, :]) * gamma_a,
                (column_sum(spread) + column_sum(straight)) * gamma_b,
                (
                    column_sum(spread * norm_b[COLS:-COLS, :])
                    + column_sum(straight * norm_b[own, :])
                )
                * gamma_b,
            ],
            axis=0,
        )
    )


def first_kernel(main, pass_a, norm_a, pass_b, norm_b, params, a_high, a_low, sums):
    parts = first_sums(main, pass_a, norm_a, pass_b, norm_b, params, a_high, a_low)
    sums[...] = jnp.broadcast_to(parts[None], sums.shape)


def sharing_kernel(share, main, pass_a, norm_a, pass_b, norm_b, params, a_high, a_low, sums):
    parts = first_sums(main, pass_a, norm_a, pass_b, norm_b, params, a_high, a_low)
    parts = jnp.concatenate([parts, share[...]], axis=0)
    sums[...] = jnp.broadcast_to(parts[None], sums.shape)


def through(incoming, passing, normed, inside, gamma, inverse, means, high, low):
    grad = inverse * (incoming * passing * gamma - inside * means[0:1] - normed * means[1:2])
    return grad, incoming[COLS:-COLS] + conv_back(grad, high, low)


def gain_sums(grad_out, normed):
    return jnp.concatenate([column_sum(grad_out * normed), column_sum(grad_out)], axis=0)


def opening_kernel(
    tiles, flags, opening, above, main, below, response, pass_a, norm_a, pass_b, norm_b,
    params, a_high, a_low, sums, middle, grad_a, gain_a,
):
    incoming = jnp.concatenate(
        [above[5 * COLS :, :], main[...], below[5 * COLS :, :]], axis=0
    )
    grad, passed = through(
        incoming, pass_a[...], norm_a[...], inside_rows(flags, tiles),
        params[0:1, :], params[1:2, :], opening[...], a_high, a_low,
    )
    middle[...] = passed
    grad_a[...] = grad[2 * COLS : -2 * COLS]
    own = slice(2 * COLS, 2 * COLS + OWN)
    gain_a[...] = gain_sums(main[...] * pass_a[own, :], norm_a[own, :])
    grad_b = passed[COLS:-COLS] * pass_b[own, :]
    gamma_b = params[2:3, :]
    packed = pack(
        jnp.concatenate(
            [
                jnp.zeros((2, C), f32),
                column_sum(grad_b) * gamma_b,
                column_sum(grad_b * norm_b[own, :]) * gamma_b,
            ],
            axis=0,
        )
    )
    sums[:, 0:1, :] = jnp.broadcast_to(packed[None], (tiles, 1, LANES))
    if tiles == GROUPS:
        sums[:, 1, :] = response[...]
    else:
        sums[:, 1:, :] = response[...].reshape(tiles, GROUPS // tiles, LANES)


def closing_kernel(
    count, tiles, flags, received, middle, grad_a, gain_a, pass_b, norm_b, params, b_high, b_low,
    out, out_head, out_tail, act, grad, gain, share,
):
    share[...] = jnp.sum(received[:, 1:, :], axis=0)
    means = unpack(jnp.sum(received[:, 0:1, :], axis=0) * (1.0 / count))[2:4]
    near = middle[...]
    grad_b, last = through(
        near, pass_b[COLS:-COLS, :], norm_b[COLS:-COLS, :],
        inside_rows(flags, tiles)[COLS:-COLS], params[2:3, :], params[3:4, :],
        means, b_high, b_low,
    )
    out[...] = last
    out_head[...] = last[: 2 * COLS]
    out_tail[...] = last[-2 * COLS :]
    active = flags[0] == 0
    upper = flags[1] == 1
    own = slice(2 * COLS, 2 * COLS + OWN)
    gain_b = gain_sums(near[COLS:-COLS] * pass_b[own, :], norm_b[own, :])
    act[...] = jnp.where(active, jnp.where(upper, near[COLS:-COLS], last), 0.0)
    grad[...] = jnp.where(active, jnp.where(upper, grad_a[...], grad_b[COLS:-COLS]), 0.0)
    gain[...] = jnp.where(active, jnp.where(upper, gain_a[...], gain_b), 0.0)


def second_kernel(
    count, tiles, step, flags, received, exchanged, top, main, bottom, pass_a, norm_a, pass_b, norm_b,
    params, a_high, a_low, b_high, b_low, old_act, old_grad, old_gain,
    out, out_head, out_tail, act, grad, gain,
):
    incoming = jnp.concatenate([top[...], main[...], bottom[...]], axis=0)
    means = jnp.sum(received[:, 0:1, :], axis=0) * (1.0 / count)
    if tiles == GROUPS:
        response = exchanged[:, 1, :]
    else:
        response = exchanged[:, 1:, :].reshape(GROUPS, LANES)
    right = lane_quarter(GROUPS) >= 2
    response = jnp.concatenate(
        [
            jnp.where(right, pltpu.roll(response, 2 * GROUPS, 1), 0.0),
            jnp.where(right, response, 0.0),
            jnp.zeros((2 * GROUPS, LANES), f32),
        ],
        axis=0,
    )
    means_a = unpack(means)[0:2]
    means_b = unpack(means - dot(means, response, highest))[2:4]
    inside = inside_rows(flags, tiles)
    grad_a, middle = through(
        incoming, pass_a[...], norm_a[...], inside, params[0:1, :], params[1:2, :],
        means_a, a_high, a_low,
    )
    grad_b, last = through(
        middle, pass_b[COLS:-COLS, :], norm_b[COLS:-COLS, :], inside[COLS:-COLS],
        params[2:3, :], params[3:4, :], means_b, b_high, b_low,
    )
    out[...] = last
    out_head[...] = last[: 2 * COLS]
    out_tail[...] = last[-2 * COLS :]
    active = flags[0] == step
    upper = flags[1] == 1
    own = slice(2 * COLS, 2 * COLS + OWN)
    gain_a = gain_sums(main[...] * pass_a[own, :], norm_a[own, :])
    gain_b = gain_sums(middle[COLS:-COLS] * pass_b[own, :], norm_b[own, :])
    act[...] = jnp.where(active, jnp.where(upper, middle[COLS:-COLS], last), old_act[...])
    grad[...] = jnp.where(
        active, jnp.where(upper, grad_a[2 * COLS : -2 * COLS], grad_b[COLS:-COLS]), old_grad[...]
    )
    gain[...] = jnp.where(active, jnp.where(upper, gain_a, gain_b), old_gain[...])


def kernel_grad_kernel(tiles, flags, above, main, below, grad, gain, mine, other):
    share = C // tiles
    image = jnp.concatenate([above[: 3 * COLS, :], main[...], below[: 3 * COLS, :]], axis=0)
    turned = grad[...].T.reshape(tiles // 2, 2, share, OWN)
    even = turned[:, 0].reshape(C // 2, OWN)
    odd = turned[:, 1].reshape(C // 2, OWN)
    core = flags[3]
    left = split(
        jnp.concatenate(
            [jnp.where(core == 0, even, odd), jnp.where(core == 0, odd, even)], axis=0
        )
    )
    for col_tap in range(3):
        high, low = split(shifted(image, col_tap - 1))
        for row_tap in range(3):
            start = (row_tap + 2) * COLS
            product = dot3(left, (high[start : start + OWN], low[start : start + OWN]))
            where = slice((row_tap * 3 + col_tap) * C, (row_tap * 3 + col_tap + 1) * C)
            mine[:, where] = product[: C // 2]
            other[:, where] = product[C // 2 :]
    half = C // 2
    eight = jnp.concatenate([gain[:, :half], gain[:, half:], jnp.zeros((4, half), f32)], axis=0)
    copies = jnp.broadcast_to(eight[None], (half // 8, 8, half)).reshape(half, half)
    mine[:, 9 * C :] = copies
    other[:, 9 * C :] = copies


def call(body, out_shape, operands, flagged, **options):
    spec = pl.BlockSpec(memory_space=pltpu.VMEM)
    in_specs = [spec] * len(operands)
    if flagged:
        in_specs[0] = pl.BlockSpec(memory_space=pltpu.SMEM)
    many = isinstance(out_shape, tuple)
    return pl.pallas_call(
        body,
        out_shape=out_shape,
        in_specs=in_specs,
        out_specs=tuple(spec for _ in out_shape) if many else spec,
        compiler_params=pltpu.CompilerParams(vmem_limit_bytes=40 * 2**20),
        **options,
    )(*operands)


def shape(*dims, dtype=f32):
    return jax.ShapeDtypeStruct(dims, dtype)


def prepare(tiles, count, flags, kernel, pieces, gathered, fields, partner_fields):
    tap = lambda rows: pl.BlockSpec((1, rows, C), lambda i: (i, 0, 0))
    whole = lambda *dims: pl.BlockSpec(dims, lambda i: (0,) * len(dims))
    tall = 12 * COLS
    return pl.pallas_call(
        functools.partial(prepare_kernel, tiles, count),
        grid=(9,),
        out_shape=tuple(shape(9, C, C, dtype=bf16) for _ in range(4))
        + tuple(shape(tall, C) for _ in range(4))
        + (shape(8, C), shape(2, C), shape(GROUPS, LANES)),
        in_specs=[
            pl.BlockSpec(memory_space=pltpu.SMEM),
            tap(C),
            *(tap(C // 4) for _ in range(4)),
            whole(*gathered.shape),
            whole(*fields.shape),
            whole(*fields.shape),
        ],
        out_specs=tuple(tap(C) for _ in range(4))
        + tuple(whole(tall, C) for _ in range(4))
        + (whole(8, C), whole(2, C), whole(GROUPS, LANES)),
        scratch_shapes=[
            pltpu.VMEM((2 * C, OWN), bf16),
            pltpu.VMEM((2 * C, OWN), bf16),
            pltpu.VMEM((3, tall, C + C // 2), f32),
            pltpu.VMEM((2 * C, C), f32),
            pltpu.VMEM((2 * C, C), f32),
        ],
        compiler_params=pltpu.CompilerParams(vmem_limit_bytes=40 * 2**20),
    )(flags, kernel, *pieces, gathered, fields, partner_fields)


def on_device(acts, kernels, gammas, pass_mask, drop_mask, path_mask, cotangent):
    pairs = lax.axis_size("pair")
    tiles = lax.axis_size(TILE)
    devices = 2 * pairs * tiles
    pair, member, core = (lax.axis_index(a) for a in ("pair", "member", "core"))
    tile = lax.axis_index(TILE)
    count = tiles * OWN * (C // GROUPS)
    swap = [(0, 1), (1, 0)]

    image = acts[0, 0].reshape(OWN, C)
    start = cotangent[0].reshape(OWN, C)
    passing, tail, head = call(
        edge_kernel,
        (shape(OWN, C), shape(7 * COLS, C), shape(7 * COLS, C)),
        (path_mask, image, pass_mask[0, 0].reshape(OWN, C), drop_mask[0, 0], start),
        True,
    )

    own_kernel = kernels[0].reshape(9, C, C)
    quarters = [
        lax.dynamic_slice_in_dim(own_kernel, core * (C // 2) + q * (C // 4), C // 4, axis=1)
        for q in range(2)
    ]
    layers = lax.axis_size("z")
    route = [(i, layers + i) for i in range(layers)] + [(layers + i, i) for i in range(layers)]
    route_two = [(i, layers + (i - 1) % layers) for i in range(layers)] + [
        (layers + (i - 1) % layers, i) for i in range(layers)
    ]
    near = lax.ppermute(quarters[0], ("member", "z"), route)
    near_two = lax.ppermute(quarters[1], ("member", "z"), route_two)
    flags = jnp.stack([pairs - 1 - pair, member, tile, core]).astype(jnp.int32)

    def neighbours(value, step, source=None):
        size = 2 * tiles
        first, last, jump = (0, devices, 0) if source is None else (
            source * size, (source + 1) * size, size,
        )
        return lax.ppermute(
            value,
            ALL,
            [
                (i, i - jump + step)
                for i in range(first, last)
                if 0 <= i % tiles + step < tiles
            ],
        )

    from_above = neighbours(tail, 1)
    from_below = neighbours(head, -1)
    tall = 12 * COLS
    edges = (from_above, image, from_below)
    fields, sums = call(
        forward_kernel,
        (shape(2 * tall + 8, C), shape(2 * tiles, 1, LANES)),
        edges + (passing, start, own_kernel, gammas),
        False,
    )
    partner_fields = lax.ppermute(fields, "member", swap)
    gathered = lax.all_to_all(sums, ("member",) + TILE, 0, 0)
    near, near_two, gathered, partner_fields = lax.optimization_barrier(
        (near, near_two, gathered, partner_fields)
    )
    far = lax.ppermute(near, "core", swap)
    far_two = lax.ppermute(near_two, "core", swap)
    prepared = prepare(
        tiles, count, flags, own_kernel, (near, near_two, far, far_two), gathered, fields,
        partner_fields,
    )
    a_high, a_low, b_high, b_low = (w.reshape(3, 3 * C, C) for w in prepared[:4])
    masks, params, opening, response = prepared[4:8], prepared[8], prepared[9], prepared[10]
    piece = GROUPS // tiles
    block = 1 + piece
    shared = masks + (params, a_high, a_low)
    rows_out = (
        shape(OWN, C),
        shape(2 * COLS, C),
        shape(2 * COLS, C),
        shape(OWN, C),
        shape(OWN, C),
        shape(2, C),
    )

    sums, middle, grad_a, gain_a = call(
        functools.partial(opening_kernel, tiles),
        (shape(tiles, block, LANES), shape(OWN + 2 * COLS, C), shape(OWN, C), shape(2, C)),
        (flags, opening, from_above, start, from_below, response) + shared,
        True,
    )
    received = lax.all_to_all(sums, TILE, 0, 0)
    main, head, tail, act, grad, gain, share = call(
        functools.partial(closing_kernel, count, tiles),
        rows_out + (shape(piece, LANES),),
        (flags, received, middle, grad_a, gain_a) + masks[2:] + (params, b_high, b_low),
        True,
    )
    exchanged = None
    for step in range(1, pairs):
        main, top, bottom = (
            neighbours(main, 0, pairs - step),
            neighbours(tail, 1, pairs - step),
            neighbours(head, -1, pairs - step),
        )
        if step == 1:
            sums = call(sharing_kernel, shape(tiles, block, LANES), (share, main) + shared, False)
        else:
            sums = call(first_kernel, shape(tiles, 1, LANES), (main,) + shared, False)
        sums, top, bottom = lax.optimization_barrier((sums, top, bottom))
        received = lax.all_to_all(sums, TILE, 0, 0)
        if step == 1:
            exchanged = received
        main, head, tail, act, grad, gain = call(
            functools.partial(second_kernel, count, tiles, step),
            rows_out,
            (flags, received, exchanged, top, main, bottom)
            + shared
            + (b_high, b_low, act, grad, gain),
            True,
        )

    width = 9 * C + C // 2
    mine, other = call(
        functools.partial(kernel_grad_kernel, tiles),
        (shape(C // 2, width), shape(C // 2, width)),
        (flags,) + edges + (grad, gain),
        True,
    )
    mine = mine + lax.ppermute(other, "core", swap)
    for axis in ("x", "z"):
        parts = lax.axis_size(axis)
        mine = jnp.sum(
            lax.all_to_all(mine.reshape(parts, mine.shape[0] // parts, width), axis, 0, 0), axis=0
        )
    kernel_share = jnp.transpose(mine[:, : 9 * C].reshape(C // tiles, 3, 3, C), (1, 2, 3, 0))
    gain = jnp.concatenate([mine[0:2, 9 * C :], mine[2:4, 9 * C :]], axis=1)
    return (
        act.reshape(1, 1, ROWS, COLS, C),
        kernel_share[None],
        gain[None],
    )


def solution(mesh):
    sections, tiles = mesh.shape["section"], mesh.shape["tile"]
    across = min(4, tiles // 2)
    finer = Mesh(
        mesh.devices.reshape(sections // 2, 2, tiles // (2 * across), across, 2), ALL
    )
    return jax.shard_map(
        on_device,
        mesh=finer,
        in_specs=(
            P(SECTION, None, TILE, None, None),
            P(SECTION, None, None, None, None),
            P(SECTION, None),
            P(SECTION, None, TILE, None, None),
            P(SECTION, None, TILE, None),
            P(SECTION, None),
            P(None, TILE, None, None),
        ),
        out_specs=(
            P(SECTION, None, TILE, None, None),
            P(SECTION, None, None, None, TILE),
            P(SECTION, None, None),
        ),
        check_vma=False,
    )
```

```python
import functools

import jax
import jax.numpy as jnp
from jax import lax
from jax.experimental import pallas as pl
from jax.experimental.pallas import tpu as pltpu
from jax.sharding import Mesh
from jax.sharding import PartitionSpec as P

GROUPS = 32
C = 256
COLS = 16
ROWS = 8
OWN = ROWS * COLS
LANES = 4 * GROUPS

keep_drop = 0.9
keep_path = 0.75
eps = 1e-05
highest = lax.Precision.HIGHEST
f32 = jnp.float32
bf16 = jnp.bfloat16

SECTION = ("pair", "member")
TILE = ("x", "z", "core")
ALL = SECTION + TILE


def split(values):
    high = values.astype(bf16)
    return high, (values - high.astype(f32)).astype(bf16)


def dot(left, right, precision=None):
    return jnp.dot(left, right, preferred_element_type=f32, precision=precision)


def dot3(left, right):
    lh, ll = left
    rh, rl = right
    return dot(lh, rh) + dot(ll, rh) + dot(lh, rl)


def shifted(values, offset):
    if offset == 0:
        return values
    count = values.shape[0]
    column = lax.broadcasted_iota(jnp.int32, values.shape, 0) & (COLS - 1)
    rolled = pltpu.roll(values, (-offset) % count, 0)
    edge = COLS - 1 if offset > 0 else 0
    return jnp.where(column == edge, 0.0, rolled)


def conv_back(field, high_ref, low_ref):
    wide = jnp.concatenate([shifted(field, 1), field, shifted(field, -1)], axis=1)
    high, low = split(wide)
    count = field.shape[0] - 2 * COLS
    total = None
    for tap in range(3):
        start = (2 - tap) * COLS
        part = dot3(
            (high[start : start + count], low[start : start + count]),
            (high_ref[tap], low_ref[tap]),
        )
        total = part if total is None else total + part
    return total


def group_matrix(width=GROUPS, first=0):
    channel = lax.broadcasted_iota(jnp.int32, (C, width), 0)
    group = lax.broadcasted_iota(jnp.int32, (C, width), 1)
    return jnp.where((channel >> 3) + first == group, 1.0, 0.0).astype(f32)


def exact_dot(left, right):
    count = left.shape[0]
    high = left.astype(bf16)
    rest = left - high.astype(f32)
    middle = rest.astype(bf16)
    low = (rest - middle.astype(f32)).astype(bf16)
    pieces = jnp.concatenate([x.astype(f32) for x in (high, middle, low)], axis=0).astype(bf16)
    product = dot(pieces, right.astype(bf16))
    return product[:count] + product[count : 2 * count] + product[2 * count :]


def lane_quarter(rows):
    return lax.broadcasted_iota(jnp.int32, (rows, LANES), 1) >> 5


def repeated_groups():
    channel = lax.broadcasted_iota(jnp.int32, (C, LANES), 0)
    lane = lax.broadcasted_iota(jnp.int32, (C, LANES), 1)
    return jnp.where((channel >> 3) == (lane & (GROUPS - 1)), 1.0, 0.0)


def pack(rows):
    sums = exact_dot(rows, repeated_groups())
    row = lax.broadcasted_iota(jnp.int32, (4, LANES), 0)
    return column_sum(jnp.where(lane_quarter(4) == row, sums, 0.0))


def unpack(packed):
    row = lax.broadcasted_iota(jnp.int32, (4, LANES), 0)
    apart = jnp.where(lane_quarter(4) == row, jnp.broadcast_to(packed, (4, LANES)), 0.0)
    lane = lax.broadcasted_iota(jnp.int32, (LANES, C), 0)
    channel = lax.broadcasted_iota(jnp.int32, (LANES, C), 1)
    return exact_dot(apart, jnp.where((channel >> 3) == (lane & (GROUPS - 1)), 1.0, 0.0))


def column_sum(values):
    return jnp.sum(values, axis=0, keepdims=True)


def edge_kernel(path, image, mask, drop, start, passing, tail, head):
    pixel = lax.broadcasted_iota(jnp.int32, (OWN, ROWS), 0)
    row = lax.broadcasted_iota(jnp.int32, (OWN, ROWS), 1)
    by_row = dot(
        jnp.where((pixel >> 4) == row, 1.0, 0.0).astype(bf16), drop[...].astype(f32).astype(bf16)
    )
    pixel = lax.broadcasted_iota(jnp.int32, (OWN, COLS), 0)
    column = lax.broadcasted_iota(jnp.int32, (OWN, COLS), 1)
    kept = jnp.sum(jnp.where((pixel & (COLS - 1)) == column, by_row, 0.0), axis=1, keepdims=True)
    kept_path = path[0, 0].astype(f32) / keep_path
    values = mask[...].astype(f32) * (kept / keep_drop) * kept_path
    passing[...] = values
    tail[: 3 * COLS, :] = image[-3 * COLS :, :]
    tail[3 * COLS : 5 * COLS, :] = values[-2 * COLS :]
    tail[5 * COLS :, :] = start[-2 * COLS :, :]
    head[: 3 * COLS, :] = image[: 3 * COLS, :]
    head[3 * COLS : 5 * COLS, :] = values[: 2 * COLS]
    head[5 * COLS :, :] = start[: 2 * COLS, :]


def forward_kernel(above, main, below, passing, start, kernel, gamma, fields, sums):
    image = jnp.concatenate([above[: 3 * COLS, :], main[...], below[: 3 * COLS, :]], axis=0)
    count = tall = image.shape[0] - 2 * COLS
    total = None
    for col_tap in range(3):
        high, low = split(shifted(image, col_tap - 1))
        for row_tap in range(3):
            start_row = row_tap * COLS
            part = dot3(
                (high[start_row : start_row + count], low[start_row : start_row + count]),
                split(kernel[row_tap * 3 + col_tap]),
            )
            total = part if total is None else total + part
    fields[:tall, :] = total
    fields[tall : 2 * tall, :] = jnp.concatenate(
        [above[3 * COLS : 5 * COLS, :], passing[...], below[3 * COLS : 5 * COLS, :]], axis=0
    )
    fields[2 * tall :, :] = jnp.concatenate([gamma[...], jnp.zeros((7, C), f32)], axis=0)
    own = total[2 * COLS : 2 * COLS + OWN]
    grad_out = start[...] * passing[...]
    packed = pack(
        jnp.concatenate(
            [
                column_sum(own),
                column_sum(own * own),
                column_sum(grad_out) * gamma[...],
                column_sum(grad_out * own) * gamma[...],
            ],
            axis=0,
        )
    )
    sums[...] = jnp.broadcast_to(packed[None], sums.shape)


def prepare_kernel(
    tiles, count, flags, own, near, near_two, far, far_two, gathered, fields, partner_fields,
    a_high, a_low, b_high, b_low, pass_a, norm_a, pass_b, norm_b, params, opening, response,
    high_scr, low_scr, field_scr, flat_scr, full_scr,
):
    row_tap = pl.program_id(0)
    core = flags[3]
    member = flags[1]

    @pl.when(row_tap == 0)
    def _():
        stats = [
            jnp.sum(gathered[which * tiles : (which + 1) * tiles], axis=0) * (1.0 / count)
            for which in range(2)
        ]
        inside = inside_rows(flags, tiles)
        tall = 12 * COLS

        def section(which, conv_out, passing, gamma, pass_ref, norm_ref, row):
            wide = unpack(stats[which])
            mean, square = wide[0:1], wide[1:2]
            inverse = lax.rsqrt(square - mean * mean + eps)
            pass_ref[...] = passing
            norm_ref[...] = (conv_out - mean) * inverse * inside
            params[row : row + 1, :] = gamma
            params[row + 1 : row + 2, :] = inverse
            if which == 1:
                opening[0:1, :] = wide[2:3]
                opening[1:2, :] = inverse * (wide[3:4] - mean * wide[2:3])

        upper = member == 1
        mine, other = fields[:tall, :], partner_fields[:tall, :]
        my_pass, other_pass = fields[tall : 2 * tall, :], partner_fields[tall : 2 * tall, :]
        my_gamma = fields[2 * tall : 2 * tall + 1, :]
        other_gamma = partner_fields[2 * tall : 2 * tall + 1, :]
        section(1, jnp.where(upper, mine, other), jnp.where(upper, my_pass, other_pass),
                jnp.where(upper, my_gamma, other_gamma), pass_a, norm_a, 0)
        section(0, jnp.where(upper, other, mine), jnp.where(upper, other_pass, my_pass),
                jnp.where(upper, other_gamma, my_gamma), pass_b, norm_b, 2)
        params[4:8, :] = jnp.zeros((4, C), f32)
        passing = pass_b[2 * COLS : 2 * COLS + OWN]
        normed = norm_b[2 * COLS : 2 * COLS + OWN]
        high, low = split(jnp.concatenate([passing.T, (passing * normed).T], axis=0))
        high_scr[...] = high
        low_scr[...] = low
        both = jnp.concatenate([norm_a[...], inside[:, : C // 2]], axis=1)
        field_scr[0] = shifted(both, 1)
        field_scr[1] = both
        field_scr[2] = shifted(both, -1)
        flat_scr[...] = jnp.zeros_like(flat_scr)
        full_scr[...] = jnp.zeros_like(full_scr)

    begin = pl.multiple_of((3 - row_tap) * COLS, COLS)
    for col_tap in range(3):
        near_tap = jnp.concatenate([near[col_tap], near_two[col_tap]], axis=0)
        far_tap = jnp.concatenate([far[col_tap], far_two[col_tap]], axis=0)
        partner = jnp.concatenate(
            [jnp.where(core == 0, near_tap, far_tap), jnp.where(core == 0, far_tap, near_tap)],
            axis=0,
        )
        kernel_a = jnp.where(member == 1, own[col_tap], partner)
        kernel_b = jnp.where(member == 1, partner, own[col_tap])
        high, low = split(kernel_a.T)
        a_high[col_tap] = high
        a_low[col_tap] = low
        high, low = split(kernel_b.T)
        b_high[col_tap] = high
        b_low[col_tap] = low
        moved = split(field_scr[col_tap, pl.ds(begin, OWN), :])
        moment = dot3((high_scr[...], low_scr[...]), moved)
        full_scr[:C, :] += moment[:C, :C] * kernel_a
        full_scr[C:, :] += moment[C:, :C] * kernel_a
        flat_scr[:C, :] += moment[:C, C : C + 1] * kernel_a
        flat_scr[C:, :] += moment[C:, C : C + 1] * kernel_a

    @pl.when(row_tap == 2)
    def _():
        groups = group_matrix()
        contract = (((0,), (1,)), ((), ()))
        total = jnp.zeros((GROUPS, LANES), f32)
        for index, scratch in enumerate((flat_scr, full_scr)):
            part = lax.dot_general(
                groups, scratch[...] * params[1:2, :], contract,
                preferred_element_type=f32, precision=highest,
            )
            for side in range(2):
                sums = exact_dot(
                    part[:, side * C : (side + 1) * C] * params[2:3, :], repeated_groups()
                )
                total += jnp.where(lane_quarter(GROUPS) == index * 2 + side, sums, 0.0)
        response[...] = total * (1.0 / count)


def inside_rows(flags, tiles):
    row = lax.broadcasted_iota(jnp.int32, (12 * COLS, C), 0)
    first = jnp.where(flags[2] == 0, 2 * COLS, 0)
    last = jnp.where(flags[2] == tiles - 1, 10 * COLS, 12 * COLS)
    return jnp.where((row >= first) & (row < last), 1.0, 0.0).astype(f32)


def first_sums(main, pass_a, norm_a, pass_b, norm_b, params, a_high, a_low):
    own = slice(2 * COLS, 2 * COLS + OWN)
    incoming = main[...]
    grad_out = incoming * pass_a[own, :]
    blank = jnp.zeros((2 * COLS, C), f32)
    scaled = jnp.concatenate([blank, grad_out * (params[0:1, :] * params[1:2, :]), blank], axis=0)
    spread = conv_back(scaled, a_high, a_low) * pass_b[COLS:-COLS, :]
    straight = incoming * pass_b[own, :]
    gamma_a, gamma_b = params[0:1, :], params[2:3, :]
    return pack(
        jnp.concatenate(
            [
                column_sum(grad_out) * gamma_a,
                column_sum(grad_out * norm_a[own, :]) * gamma_a,
                (column_sum(spread) + column_sum(straight)) * gamma_b,
                (
                    column_sum(spread * norm_b[COLS:-COLS, :])
                    + column_sum(straight * norm_b[own, :])
                )
                * gamma_b,
            ],
            axis=0,
        )
    )


def first_kernel(main, pass_a, norm_a, pass_b, norm_b, params, a_high, a_low, sums):
    parts = first_sums(main, pass_a, norm_a, pass_b, norm_b, params, a_high, a_low)
    sums[...] = jnp.broadcast_to(parts[None], sums.shape)


def sharing_kernel(share, main, pass_a, norm_a, pass_b, norm_b, params, a_high, a_low, sums):
    parts = first_sums(main, pass_a, norm_a, pass_b, norm_b, params, a_high, a_low)
    parts = jnp.concatenate([parts, share[...]], axis=0)
    sums[...] = jnp.broadcast_to(parts[None], sums.shape)


def through(incoming, passing, normed, inside, gamma, inverse, means, high, low):
    grad = inverse * (incoming * passing * gamma - inside * means[0:1] - normed * means[1:2])
    return grad, incoming[COLS:-COLS] + conv_back(grad, high, low)


def gain_sums(grad_out, normed):
    return jnp.concatenate([column_sum(grad_out * normed), column_sum(grad_out)], axis=0)


def opening_kernel(
    tiles, flags, opening, above, main, below, response, pass_a, norm_a, pass_b, norm_b,
    params, a_high, a_low, sums, middle, grad_a, gain_a,
):
    incoming = jnp.concatenate(
        [above[5 * COLS :, :], main[...], below[5 * COLS :, :]], axis=0
    )
    grad, passed = through(
        incoming, pass_a[...], norm_a[...], inside_rows(flags, tiles),
        params[0:1, :], params[1:2, :], opening[...], a_high, a_low,
    )
    middle[...] = passed
    grad_a[...] = grad[2 * COLS : -2 * COLS]
    own = slice(2 * COLS, 2 * COLS + OWN)
    gain_a[...] = gain_sums(main[...] * pass_a[own, :], norm_a[own, :])
    grad_b = passed[COLS:-COLS] * pass_b[own, :]
    gamma_b = params[2:3, :]
    packed = pack(
        jnp.concatenate(
            [
                jnp.zeros((2, C), f32),
                column_sum(grad_b) * gamma_b,
                column_sum(grad_b * norm_b[own, :]) * gamma_b,
            ],
            axis=0,
        )
    )
    sums[:, 0:1, :] = jnp.broadcast_to(packed[None], (tiles, 1, LANES))
    if tiles == GROUPS:
        sums[:, 1, :] = response[...]
    else:
        sums[:, 1:, :] = response[...].reshape(tiles, GROUPS // tiles, LANES)


def closing_kernel(
    count, tiles, flags, received, middle, grad_a, gain_a, pass_b, norm_b, params, b_high, b_low,
    out, out_head, out_tail, act, grad, gain, share,
):
    share[...] = jnp.sum(received[:, 1:, :], axis=0)
    means = unpack(jnp.sum(received[:, 0:1, :], axis=0) * (1.0 / count))[2:4]
    near = middle[...]
    grad_b, last = through(
        near, pass_b[COLS:-COLS, :], norm_b[COLS:-COLS, :],
        inside_rows(flags, tiles)[COLS:-COLS], params[2:3, :], params[3:4, :],
        means, b_high, b_low,
    )
    out[...] = last
    out_head[...] = last[: 2 * COLS]
    out_tail[...] = last[-2 * COLS :]
    active = flags[0] == 0
    upper = flags[1] == 1
    own = slice(2 * COLS, 2 * COLS + OWN)
    gain_b = gain_sums(near[COLS:-COLS] * pass_b[own, :], norm_b[own, :])
    act[...] = jnp.where(active, jnp.where(upper, near[COLS:-COLS], last), 0.0)
    grad[...] = jnp.where(active, jnp.where(upper, grad_a[...], grad_b[COLS:-COLS]), 0.0)
    gain[...] = jnp.where(active, jnp.where(upper, gain_a[...], gain_b), 0.0)


def second_kernel(
    count, tiles, step, flags, received, exchanged, top, main, bottom, pass_a, norm_a, pass_b, norm_b,
    params, a_high, a_low, b_high, b_low, old_act, old_grad, old_gain,
    out, out_head, out_tail, act, grad, gain,
):
    incoming = jnp.concatenate([top[...], main[...], bottom[...]], axis=0)
    means = jnp.sum(received[:, 0:1, :], axis=0) * (1.0 / count)
    if tiles == GROUPS:
        response = exchanged[:, 1, :]
    else:
        response = exchanged[:, 1:, :].reshape(GROUPS, LANES)
    right = lane_quarter(GROUPS) >= 2
    response = jnp.concatenate(
        [
            jnp.where(right, pltpu.roll(response, 2 * GROUPS, 1), 0.0),
            jnp.where(right, response, 0.0),
            jnp.zeros((2 * GROUPS, LANES), f32),
        ],
        axis=0,
    )
    means_a = unpack(means)[0:2]
    means_b = unpack(means - dot(means, response, highest))[2:4]
    inside = inside_rows(flags, tiles)
    grad_a, middle = through(
        incoming, pass_a[...], norm_a[...], inside, params[0:1, :], params[1:2, :],
        means_a, a_high, a_low,
    )
    grad_b, last = through(
        middle, pass_b[COLS:-COLS, :], norm_b[COLS:-COLS, :], inside[COLS:-COLS],
        params[2:3, :], params[3:4, :], means_b, b_high, b_low,
    )
    out[...] = last
    out_head[...] = last[: 2 * COLS]
    out_tail[...] = last[-2 * COLS :]
    active = flags[0] == step
    upper = flags[1] == 1
    own = slice(2 * COLS, 2 * COLS + OWN)
    gain_a = gain_sums(main[...] * pass_a[own, :], norm_a[own, :])
    gain_b = gain_sums(middle[COLS:-COLS] * pass_b[own, :], norm_b[own, :])
    act[...] = jnp.where(active, jnp.where(upper, middle[COLS:-COLS], last), old_act[...])
    grad[...] = jnp.where(
        active, jnp.where(upper, grad_a[2 * COLS : -2 * COLS], grad_b[COLS:-COLS]), old_grad[...]
    )
    gain[...] = jnp.where(active, jnp.where(upper, gain_a, gain_b), old_gain[...])


def kernel_grad_kernel(tiles, flags, above, main, below, grad, gain, mine, other):
    share = C // tiles
    image = jnp.concatenate([above[: 3 * COLS, :], main[...], below[: 3 * COLS, :]], axis=0)
    turned = grad[...].T.reshape(tiles // 2, 2, share, OWN)
    even = turned[:, 0].reshape(C // 2, OWN)
    odd = turned[:, 1].reshape(C // 2, OWN)
    core = flags[3]
    left = split(
        jnp.concatenate(
            [jnp.where(core == 0, even, odd), jnp.where(core == 0, odd, even)], axis=0
        )
    )
    for col_tap in range(3):
        high, low = split(shifted(image, col_tap - 1))
        for row_tap in range(3):
            start = (row_tap + 2) * COLS
            product = dot3(left, (high[start : start + OWN], low[start : start + OWN]))
            where = slice((row_tap * 3 + col_tap) * C, (row_tap * 3 + col_tap + 1) * C)
            mine[:, where] = product[: C // 2]
            other[:, where] = product[C // 2 :]
    half = C // 2
    eight = jnp.concatenate([gain[:, :half], gain[:, half:], jnp.zeros((4, half), f32)], axis=0)
    copies = jnp.broadcast_to(eight[None], (half // 8, 8, half)).reshape(half, half)
    mine[:, 9 * C :] = copies
    other[:, 9 * C :] = copies


def call(body, out_shape, operands, flagged, **options):
    spec = pl.BlockSpec(memory_space=pltpu.VMEM)
    in_specs = [spec] * len(operands)
    if flagged:
        in_specs[0] = pl.BlockSpec(memory_space=pltpu.SMEM)
    many = isinstance(out_shape, tuple)
    return pl.pallas_call(
        body,
        out_shape=out_shape,
        in_specs=in_specs,
        out_specs=tuple(spec for _ in out_shape) if many else spec,
        compiler_params=pltpu.CompilerParams(vmem_limit_bytes=40 * 2**20),
        **options,
    )(*operands)


def shape(*dims, dtype=f32):
    return jax.ShapeDtypeStruct(dims, dtype)


def prepare(tiles, count, flags, kernel, pieces, gathered, fields, partner_fields):
    tap = lambda rows: pl.BlockSpec((3, rows, C), lambda i: (i, 0, 0))
    whole = lambda *dims: pl.BlockSpec(dims, lambda i: (0,) * len(dims))
    tall = 12 * COLS
    return pl.pallas_call(
        functools.partial(prepare_kernel, tiles, count),
        grid=(3,),
        out_shape=tuple(shape(9, C, C, dtype=bf16) for _ in range(4))
        + tuple(shape(tall, C) for _ in range(4))
        + (shape(8, C), shape(2, C), shape(GROUPS, LANES)),
        in_specs=[
            pl.BlockSpec(memory_space=pltpu.SMEM),
            tap(C),
            *(tap(C // 4) for _ in range(4)),
            whole(*gathered.shape),
            whole(*fields.shape),
            whole(*fields.shape),
        ],
        out_specs=tuple(tap(C) for _ in range(4))
        + tuple(whole(tall, C) for _ in range(4))
        + (whole(8, C), whole(2, C), whole(GROUPS, LANES)),
        scratch_shapes=[
            pltpu.VMEM((2 * C, OWN), bf16),
            pltpu.VMEM((2 * C, OWN), bf16),
            pltpu.VMEM((3, tall, C + C // 2), f32),
            pltpu.VMEM((2 * C, C), f32),
            pltpu.VMEM((2 * C, C), f32),
        ],
        compiler_params=pltpu.CompilerParams(vmem_limit_bytes=40 * 2**20),
    )(flags, kernel, *pieces, gathered, fields, partner_fields)


def on_device(acts, kernels, gammas, pass_mask, drop_mask, path_mask, cotangent):
    pairs = lax.axis_size("pair")
    tiles = lax.axis_size(TILE)
    devices = 2 * pairs * tiles
    pair, member, core = (lax.axis_index(a) for a in ("pair", "member", "core"))
    tile = lax.axis_index(TILE)
    count = tiles * OWN * (C // GROUPS)
    swap = [(0, 1), (1, 0)]

    image = acts[0, 0].reshape(OWN, C)
    start = cotangent[0].reshape(OWN, C)
    passing, tail, head = call(
        edge_kernel,
        (shape(OWN, C), shape(7 * COLS, C), shape(7 * COLS, C)),
        (path_mask, image, pass_mask[0, 0].reshape(OWN, C), drop_mask[0, 0], start),
        True,
    )

    own_kernel = kernels[0].reshape(9, C, C)
    quarters = [
        lax.dynamic_slice_in_dim(own_kernel, core * (C // 2) + q * (C // 4), C // 4, axis=1)
        for q in range(2)
    ]
    layers = lax.axis_size("z")
    route = [(i, layers + i) for i in range(layers)] + [(layers + i, i) for i in range(layers)]
    route_two = [(i, layers + (i - 1) % layers) for i in range(layers)] + [
        (layers + (i - 1) % layers, i) for i in range(layers)
    ]
    near = lax.ppermute(quarters[0], ("member", "z"), route)
    near_two = lax.ppermute(quarters[1], ("member", "z"), route_two)
    flags = jnp.stack([pairs - 1 - pair, member, tile, core]).astype(jnp.int32)

    def neighbours(value, step, source=None):
        size = 2 * tiles
        first, last, jump = (0, devices, 0) if source is None else (
            source * size, (source + 1) * size, size,
        )
        return lax.ppermute(
            value,
            ALL,
            [
                (i, i - jump + step)
                for i in range(first, last)
                if 0 <= i % tiles + step < tiles
            ],
        )

    from_above = neighbours(tail, 1)
    from_below = neighbours(head, -1)
    tall = 12 * COLS
    edges = (from_above, image, from_below)
    fields, sums = call(
        forward_kernel,
        (shape(2 * tall + 8, C), shape(2 * tiles, 1, LANES)),
        edges + (passing, start, own_kernel, gammas),
        False,
    )
    partner_fields = lax.ppermute(fields, "member", swap)
    gathered = lax.all_to_all(sums, ("member",) + TILE, 0, 0)
    near, near_two, gathered, partner_fields = lax.optimization_barrier(
        (near, near_two, gathered, partner_fields)
    )
    far = lax.ppermute(near, "core", swap)
    far_two = lax.ppermute(near_two, "core", swap)
    prepared = prepare(
        tiles, count, flags, own_kernel, (near, near_two, far, far_two), gathered, fields,
        partner_fields,
    )
    a_high, a_low, b_high, b_low = (w.reshape(3, 3 * C, C) for w in prepared[:4])
    masks, params, opening, response = prepared[4:8], prepared[8], prepared[9], prepared[10]
    piece = GROUPS // tiles
    block = 1 + piece
    shared = masks + (params, a_high, a_low)
    rows_out = (
        shape(OWN, C),
        shape(2 * COLS, C),
        shape(2 * COLS, C),
        shape(OWN, C),
        shape(OWN, C),
        shape(2, C),
    )

    sums, middle, grad_a, gain_a = call(
        functools.partial(opening_kernel, tiles),
        (shape(tiles, block, LANES), shape(OWN + 2 * COLS, C), shape(OWN, C), shape(2, C)),
        (flags, opening, from_above, start, from_below, response) + shared,
        True,
    )
    received = lax.all_to_all(sums, TILE, 0, 0)
    main, head, tail, act, grad, gain, share = call(
        functools.partial(closing_kernel, count, tiles),
        rows_out + (shape(piece, LANES),),
        (flags, received, middle, grad_a, gain_a) + masks[2:] + (params, b_high, b_low),
        True,
    )
    exchanged = None
    for step in range(1, pairs):
        main, top, bottom = (
            neighbours(main, 0, pairs - step),
            neighbours(tail, 1, pairs - step),
            neighbours(head, -1, pairs - step),
        )
        if step == 1:
            sums = call(sharing_kernel, shape(tiles, block, LANES), (share, main) + shared, False)
        else:
            sums = call(first_kernel, shape(tiles, 1, LANES), (main,) + shared, False)
        sums, top, bottom = lax.optimization_barrier((sums, top, bottom))
        received = lax.all_to_all(sums, TILE, 0, 0)
        if step == 1:
            exchanged = received
        main, head, tail, act, grad, gain = call(
            functools.partial(second_kernel, count, tiles, step),
            rows_out,
            (flags, received, exchanged, top, main, bottom)
            + shared
            + (b_high, b_low, act, grad, gain),
            True,
        )

    width = 9 * C + C // 2
    mine, other = call(
        functools.partial(kernel_grad_kernel, tiles),
        (shape(C // 2, width), shape(C // 2, width)),
        (flags,) + edges + (grad, gain),
        True,
    )
    mine = mine + lax.ppermute(other, "core", swap)
    for axis in ("x", "z"):
        parts = lax.axis_size(axis)
        mine = jnp.sum(
            lax.all_to_all(mine.reshape(parts, mine.shape[0] // parts, width), axis, 0, 0), axis=0
        )
    kernel_share = jnp.transpose(mine[:, : 9 * C].reshape(C // tiles, 3, 3, C), (1, 2, 3, 0))
    gain = jnp.concatenate([mine[0:2, 9 * C :], mine[2:4, 9 * C :]], axis=1)
    return (
        act.reshape(1, 1, ROWS, COLS, C),
        kernel_share[None],
        gain[None],
    )


def solution(mesh):
    sections, tiles = mesh.shape["section"], mesh.shape["tile"]
    across = min(4, tiles // 2)
    finer = Mesh(
        mesh.devices.reshape(sections // 2, 2, tiles // (2 * across), across, 2), ALL
    )
    return jax.shard_map(
        on_device,
        mesh=finer,
        in_specs=(
            P(SECTION, None, TILE, None, None),
            P(SECTION, None, None, None, None),
            P(SECTION, None),
            P(SECTION, None, TILE, None, None),
            P(SECTION, None, TILE, None),
            P(SECTION, None),
            P(None, TILE, None, None),
        ),
        out_specs=(
            P(SECTION, None, TILE, None, None),
            P(SECTION, None, None, None, TILE),
            P(SECTION, None, None),
        ),
        check_vma=False,
    )
```
